32 devices in a mesh: grp: 2 (over y), blk: 8 (over z, x), chan: 2 (over core).
Axes of the slice: x: 2, y: 2, z: 4, core: 2. Of those that a mesh axis runs over, the one named last changes fastest.
Arguments:
- record: bfloat16 [16, 10000, 191], P(('grp', 'blk'), 'chan'), parts along dimension 0, may hold values from -300 to 300, as said below
- templates: bfloat16 [8, 512, 128], P('blk', 'chan'), may hold values from -6 to 6
- offsets: int32 [8], P('blk'), may hold values from 0 to 9488
- valid_counts: int32 [8], P('blk'), may hold values from 256 to 512
Outputs:
- detection: float32 [16, 8, 64], P(('grp', 'blk'), None, 'chan'), parts along dimension 0
The draws below stay inside these ranges and needn't reach their ends.
There are 2 independent parts, one for each index of `grp`. The reference program is written for one: setup_inputs(seed, part) draws one part's arguments, and reference() takes and returns one part's arrays. A program takes and returns all parts, laid end to end along the dimension named above; an argument that names none is the same for every part. Nothing has to cross between parts.
Inputs may be any that keep to these rules, and one draw needn't show every extreme that they name: Each record value comes from a noise draw scaled by a channel gain and a time envelope.
All inputs are finite; a program needn't handle non-finite values.
Results may differ from the reference program's by a relative error of at most 0.005.
Values may be sent and summed in bfloat16 or wider, within the bound.
No kernel may reach another device: no remote copies, remote signals or barrier semaphores. Data moves between devices by JAX's collectives and lax.ppermute only.
A program may use at most 64 MiB of HBM per device.

```python
import math
import jax
import jax.numpy as jnp
from jax import lax

CH = 10000
FP = 512
TAPS = 128
SAMPLES = 191
NCHUNK = 8
TEMPLATES = 8


def draw_record(key, part):
    key = jax.random.fold_in(key, 7)
    first, second, third = jax.random.split(key, 3)
    blocks = -(-SAMPLES // 32)
    noise = jnp.clip(jax.random.normal(first, (NCHUNK, CH, SAMPLES), jnp.float32), -5.0, 5.0)
    gains = jnp.exp(jax.random.uniform(second, (1, CH, 1), jnp.float32, math.log(0.3), math.log(3.0)))
    envelope = jnp.exp(jax.random.uniform(third, (NCHUNK, CH, blocks), jnp.float32, 0.0, math.log(10.0)))
    envelope = jnp.repeat(envelope, 32, axis=2)[:, :, :SAMPLES]
    return (noise * gains * envelope).astype(jnp.bfloat16)


def set_ends(entries, stream_key, least, high):
    shape = entries.shape
    spot = [jax.random.randint(jax.random.fold_in(stream_key, axis), (), 0, shape[axis]) for axis in range(len(shape))]
    entries = entries.at[tuple(spot)].set(least)
    longest = shape.index(max(shape))
    spot[longest] = (spot[longest] + 1) % shape[longest]
    return entries.at[tuple(spot)].set(high)


def levels(key, extent, pieces, smallest, high):
    level = 1.0
    for axis_at, shards_of in pieces:
        steps = jax.random.uniform(jax.random.fold_in(jax.random.fold_in(key, 6), axis_at), (shards_of,), jnp.float32, smallest / len(pieces), high / len(pieces))
        level = level * jnp.repeat(jnp.exp(steps), extent[axis_at] // shards_of).reshape((-1,) + (1,) * (len(extent) - 1 - axis_at))
    return level


def centred(stream_key, shape, width, limit, cuts=(), kind=jnp.bfloat16):
    gain = levels(stream_key, shape, cuts, -0.22, 0.18) if cuts else 1.0
    entries = jax.random.normal(stream_key, shape, jnp.float32) * width * gain
    return jnp.minimum(jnp.maximum(entries, -limit), limit).astype(kind)


def setup_inputs(seed: int = 0, part: int = 0) -> dict:
    splits = jax.random.split(jax.random.key(seed), 5)
    part_keys = jax.random.split(jax.random.fold_in(splits[4], part), 5)
    return {
        "record": draw_record(jax.random.fold_in(jax.random.fold_in(splits[4], part), 71), part),
        "templates": centred(splits[1], (TEMPLATES, FP, TAPS), 1.0, 6.0, ((0, 8), (1, 2))),
        "offsets": set_ends(jax.random.randint(splits[2], (TEMPLATES,), 0, CH - FP + 1), jax.random.fold_in(splits[2], 1), 0, CH - FP).astype(jnp.int32),
        "valid_counts": set_ends(jax.random.randint(splits[3], (TEMPLATES,), FP // 2, FP + 1), jax.random.fold_in(splits[3], 1), FP // 2, FP).astype(jnp.int32),
    }


def sliding_scale(record):
    squares = record.astype(jnp.float32) ** 2
    dims = squares.ndim
    window = lax.reduce_window(squares, jnp.zeros((), squares.dtype), lax.add, (1,) * (dims - 1) + (TAPS,), (1,) * dims, 'VALID')
    return lax.rsqrt(window / TAPS + 1e-06)

def correlate(data_rows, kernel):
    return lax.conv_general_dilated(data_rows, kernel[:, None, :], (1,), 'VALID', dimension_numbers=('NCH', 'OIH', 'NCH'), feature_group_count=kernel.shape[0], preferred_element_type=jnp.float32)

def reference(record, templates, offsets, valid_counts):
    scale = sliding_scale(record)

    def score_one(packed):
        template, offset_one, valid_one = packed
        data_rows = lax.dynamic_slice_in_dim(record, offset_one.astype(jnp.int32), FP, 1)
        row_scale = lax.dynamic_slice_in_dim(scale, offset_one.astype(jnp.int32), FP, 1)
        tscale = lax.rsqrt(lax.optimization_barrier(jnp.mean(template.astype(jnp.float32) ** 2, axis=-1)) + 1e-06)
        products = correlate(data_rows, template)
        coeffs = products * (1.0 / TAPS) * row_scale * tscale[None, :, None]
        live_rows = (jnp.arange(FP, dtype=jnp.int32) < valid_one).astype(jnp.float32)
        total = lax.optimization_barrier(jnp.sum(coeffs * live_rows[None, :, None], axis=1))
        return total * jnp.sqrt(TAPS / valid_one.astype(jnp.float32))
    result = lax.map(score_one, (templates, offsets, valid_counts))
    return jnp.transpose(result, (1, 0, 2))
```

```python
import functools

import jax
import jax.numpy as jnp
from jax import lax
from jax.experimental import pallas as pl
from jax.experimental.pallas import tpu as pltpu
from jax.sharding import PartitionSpec as P

LANES = 128
META = 16
CHUNK = 8


def pack_kernel(off_ref, cnt_ref, tmpl_ref, out_ref):
    rows, taps = tmpl_ref.shape
    out_ref[:taps, :] = jnp.transpose(tmpl_ref[...].astype(jnp.float32)).astype(out_ref.dtype)
    lane = lax.broadcasted_iota(jnp.int32, (META, rows), 1)
    off, cnt = off_ref[0], cnt_ref[0]
    digits = (off >> 8, off & 255, cnt >> 8, cnt & 255)
    meta = jnp.zeros((META, rows), jnp.int32)
    for at, digit in enumerate(digits):
        meta = jnp.where(lane == at, digit, meta)
    out_ref[taps:, :] = meta.astype(jnp.float32).astype(out_ref.dtype)


def pack(templates, offsets, counts):
    rows, taps = templates.shape
    return pl.pallas_call(
        pack_kernel,
        out_shape=jax.ShapeDtypeStruct((taps + META, rows), templates.dtype),
        in_specs=[
            pl.BlockSpec(memory_space=pltpu.SMEM),
            pl.BlockSpec(memory_space=pltpu.SMEM),
            pl.BlockSpec(memory_space=pltpu.VMEM),
        ],
        out_specs=pl.BlockSpec(memory_space=pltpu.VMEM),
        name="pack",
    )(offsets, counts, templates)


def score_kernel(channels, taps, shifts, xor, *refs):
    n = (len(refs) - 8) // 2
    rec_ref, own, other = refs[0], refs[1 : 1 + n], refs[1 + n : 1 + 2 * n]
    keep_ref, send_ref, tmpl, ints, rows_f, sums, total = refs[1 + 2 * n :]
    groups_half = own[0].shape[1] // LANES
    groups = 2 * groups_half
    chan = lax.axis_index("chan")
    base = chan * channels
    vregs = rec_ref.shape[0] // 8
    blocks = shifts // 8
    steps = taps // 8
    lane = lax.broadcasted_iota(jnp.int32, (8, LANES), 1)
    lane_row = lax.broadcasted_iota(jnp.int32, (1, LANES), 1)
    weights = jnp.where(lane_row == 0, 256.0, 0.0) + jnp.where(lane_row == 1, 1.0, 0.0)
    weights_c = jnp.where(lane_row == 2, 256.0, 0.0) + jnp.where(lane_row == 3, 1.0, 0.0)
    for i in range(n):
        meta = own[i][taps:, :LANES].astype(jnp.float32)[:1]
        ints[2 * i] = jnp.sum(meta * weights).astype(jnp.int32)
        ints[2 * i + 1] = jnp.sum(meta * weights_c).astype(jnp.int32)
        for g in range(groups_half):
            part = pl.ds(g * LANES, LANES)
            tmpl[i, chan * groups_half + g] = own[i][:taps, part].astype(jnp.float32)
            tmpl[i, (1 - chan) * groups_half + g] = other[i][:taps, part].astype(jnp.float32)
    total[...] = jnp.zeros_like(total)

    def item(index, _):
        i, g = index // groups, index % groups
        off, cnt = ints[2 * i], ints[2 * i + 1]
        first = off + g * LANES - base

        @pl.when((g * LANES < cnt) & (first > -LANES) & (first < channels))
        def _():
            tile = (first + LANES) // LANES
            turn = first + LANES - tile * LANES
            back = lax.rem(LANES - turn, LANES)
            low = rec_ref[:, pl.ds(pl.multiple_of(tile * LANES, LANES), LANES)].astype(jnp.float32)
            high = rec_ref[:, pl.ds(pl.multiple_of((tile + 1) * LANES, LANES), LANES)].astype(jnp.float32)
            wide = lax.broadcasted_iota(jnp.int32, low.shape, 1)
            mixed = jnp.where(wide < turn, high, low)
            rows_f[...] = pltpu.roll(mixed, back, 1)

            level = [rows_f[8 * m : 8 * m + 8, :] for m in range(vregs)]
            level = [v * v for v in level]
            span = 1
            while span < steps:
                level = [level[m] + level[m + span] for m in range(len(level) - span)]
                span *= 2
            for m in range(blocks + 1):
                sums[8 * m : 8 * m + 8, :] = level[m]

            def conv(q, acc):
                held = [rows_f[pl.ds(8 * m + q, 8), :] for m in range(steps + blocks - 1)]
                acc, window = list(acc[:blocks]), list(acc[blocks:])
                for b in range(blocks):
                    window[b] = window[b] + sums[pl.ds(8 * b + q, 8), :]
                for a in range(steps):
                    tap = jnp.broadcast_to(tmpl[i, g, pl.ds(8 * a + q, 1), :], (8, LANES))
                    for b in range(blocks):
                        acc[b] = acc[b] + tap * held[a + b]
                return tuple(acc) + tuple(window)

            zero = jnp.zeros((8, LANES), jnp.float32)
            out = lax.fori_loop(0, 8, conv, (zero,) * (2 * blocks))
            acc, window = out[:blocks], out[blocks:]
            energy = jnp.zeros((8, LANES), jnp.float32)
            for a in range(steps):
                t = tmpl[i, g, 8 * a : 8 * a + 8, :]
                energy = energy + t * t
            energy = jnp.sum(energy, axis=0, keepdims=True)
            ratio = jnp.full((1, LANES), taps, jnp.float32) / cnt.astype(jnp.float32)
            gain = lax.rsqrt(energy / taps + 1e-06) * jnp.sqrt(ratio) * (1.0 / taps)
            gain = jnp.where(lane_row + g * LANES < cnt, gain, 0.0)
            gain = jnp.broadcast_to(gain, (8, LANES))
            for b in range(blocks):
                scale = lax.rsqrt(window[b] / taps + 1e-06)
                total[i, 8 * b : 8 * b + 8, :] += acc[b] * scale * gain

        return 0

    lax.fori_loop(0, n * groups, item, 0)
    ones = jnp.ones((8, LANES), jnp.float32)
    half = shifts // 2
    for i in range(n):
        row = lax.dot_general(
            ones, total[i], (((1,), (1,)), ((), ())),
            precision=lax.Precision.HIGHEST, preferred_element_type=jnp.float32,
        )[:1]
        left, right = row[:, :half], row[:, half:]
        at = lax.axis_index("blk") ^ i if xor else i
        keep_ref[pl.ds(at, 1), :] = jnp.where(chan == 0, left, right)
        send_ref[pl.ds(at, 1), :] = jnp.where(chan == 0, right, left)


def score(record, own, other, channels, taps, shifts, xor):
    n = len(own)
    rows = own[0].shape[1]
    out = jax.ShapeDtypeStruct((n, shifts // 2), jnp.float32)
    vmem = pl.BlockSpec(memory_space=pltpu.VMEM)
    return pl.pallas_call(
        functools.partial(score_kernel, channels, taps, shifts, xor),
        out_shape=(out, out),
        in_specs=[vmem] * (1 + 2 * n),
        out_specs=(vmem, vmem),
        scratch_shapes=[
            pltpu.VMEM((n, 2 * rows // LANES, taps, LANES), jnp.float32),
            pltpu.SMEM((2 * n,), jnp.int32),
            pltpu.VMEM((record.shape[0], LANES), jnp.float32),
            pltpu.VMEM((shifts + 8, LANES), jnp.float32),
            pltpu.VMEM((n, shifts, LANES), jnp.float32),
        ],
        compiler_params=pltpu.CompilerParams(vmem_limit_bytes=32 * 2**20),
        cost_estimate=pl.CostEstimate(
            flops=4 * n * rows * taps * shifts, bytes_accessed=2 * record.size, transcendentals=0
        ),
        name="score",
    )(record, *own, *other)


def exchange(value, axis, size, mask):
    return lax.ppermute(value, axis, [(i, i ^ mask) for i in range(size)])


def on_device(mesh_shape, record, templates, offsets, counts):
    blk = mesh_shape["blk"]
    channels, samples = record.shape[1], record.shape[2]
    taps = templates.shape[2]
    shifts = samples - taps + 1
    packed = pack(templates[0], offsets, counts)
    if blk == CHUNK:
        held = {0: packed}
        for mask in (2, 4, 6):
            held[mask] = exchange(packed, "blk", blk, mask)
        for mask in (0, 2, 4, 6):
            held[mask + 1] = exchange(held[mask], "blk", blk, 1)
        own = [held[mask] for mask in range(blk)]
        other = [exchange(value, "chan", 2, 1) for value in own]
    else:
        every = lax.all_gather(packed, "blk", axis=0, tiled=False)
        across = exchange(every, "chan", 2, 1)
        own = [every[i] for i in range(blk)]
        other = [across[i] for i in range(blk)]
    tiles = -(-channels // LANES) + 2
    turned = jnp.pad(
        jnp.transpose(record[0]),
        ((0, -samples % 8), (LANES, tiles * LANES - LANES - channels)),
    )
    keeps, sends = [], []
    for at in range(0, blk, CHUNK):
        keep, send = score(
            turned, own[at : at + CHUNK], other[at : at + CHUNK],
            channels, taps, shifts, blk == CHUNK,
        )
        keeps.append(keep)
        sends.append(send)
    keep, send = (jnp.concatenate(v, axis=0) if len(v) > 1 else v[0] for v in (keeps, sends))
    return (keep + exchange(send, "chan", 2, 1))[None]


def solution(mesh):
    in_specs = (P(("grp", "blk"), "chan", None), P("blk", "chan", None), P("blk"), P("blk"))
    out_specs = P(("grp", "blk"), None, "chan")
    return jax.shard_map(
        functools.partial(on_device, dict(mesh.shape)),
        mesh=mesh, in_specs=in_specs, out_specs=out_specs, check_vma=False,
    )
```

```python
import functools

import jax
import jax.numpy as jnp
from jax import lax
from jax.experimental import pallas as pl
from jax.experimental.pallas import tpu as pltpu
from jax.sharding import PartitionSpec as P

LANES = 128
META = 16
CHUNK = 8


def pack_kernel(off_ref, cnt_ref, tmpl_ref, out_ref):
    rows, taps = tmpl_ref.shape
    out_ref[:taps, :] = jnp.transpose(tmpl_ref[...].astype(jnp.float32)).astype(out_ref.dtype)
    lane = lax.broadcasted_iota(jnp.int32, (META, rows), 1)
    off, cnt = off_ref[0], cnt_ref[0]
    digits = (off >> 8, off & 255, cnt >> 8, cnt & 255)
    meta = jnp.zeros((META, rows), jnp.int32)
    for at, digit in enumerate(digits):
        meta = jnp.where(lane == at, digit, meta)
    out_ref[taps:, :] = meta.astype(jnp.float32).astype(out_ref.dtype)


def pack(templates, offsets, counts):
    rows, taps = templates.shape
    return pl.pallas_call(
        pack_kernel,
        out_shape=jax.ShapeDtypeStruct((taps + META, rows), templates.dtype),
        in_specs=[
            pl.BlockSpec(memory_space=pltpu.SMEM),
            pl.BlockSpec(memory_space=pltpu.SMEM),
            pl.BlockSpec(memory_space=pltpu.VMEM),
        ],
        out_specs=pl.BlockSpec(memory_space=pltpu.VMEM),
        name="pack",
    )(offsets, counts, templates)


def score_kernel(taps, shifts, places, last, *refs):
    n = len(places)
    mine, theirs, mine_tail, theirs_tail, prev = refs[:5]
    packed = refs[5 : 5 + n]
    outs = refs[5 + n : 5 + n + (2 if last else 1)]
    tmpl, ints, slots, rows_f, sums, total, sems = refs[5 + n + len(outs) :]
    samples, channels = mine.shape
    width = packed[0].shape[1]
    groups = width // LANES
    tiles = groups + 1
    whole_tiles = channels // LANES
    chan = lax.axis_index("chan")
    vregs = rows_f.shape[0] // 8
    blocks = shifts // 8
    steps = taps // 8
    lane_row = lax.broadcasted_iota(jnp.int32, (1, LANES), 1)

    def digits(meta, at):
        weight = jnp.where(lane_row == at, 256.0, 0.0) + jnp.where(lane_row == at + 1, 1.0, 0.0)
        return jnp.sum(meta * weight).astype(jnp.int32)

    def tile_copies(i, act):
        start = ints[2 * i] + chan * width
        for half in range(2):
            local = start - half * channels
            needed = (local < channels) if half == 0 else (local + width > 0)
            for m in range(tiles):
                tile = ((local + 2 * width) >> 7) - 2 * width // LANES + m
                slot = half * tiles + m
                for source, tail, is_mine in ((mine, mine_tail, 0), (theirs, theirs_tail, 1)):
                    side = needed & ((chan == half) if is_mine == 0 else (chan != half))

                    @pl.when(side & (tile >= 0) & (tile < whole_tiles))
                    def _():
                        at = pl.multiple_of(tile * LANES, LANES)
                        copy = pltpu.make_async_copy(
                            source.at[:, pl.ds(at, LANES)], slots.at[i, slot], sems.at[i, slot]
                        )
                        if act == "start":
                            copy.start()
                        else:
                            copy.wait()

                    if act == "start" and channels % LANES:

                        @pl.when(side & (tile == whole_tiles))
                        def _():
                            slots[i, slot] = tail[...]

    for i in range(n):
        meta = packed[i][taps:, :LANES].astype(jnp.float32)[:1]
        ints[2 * i] = digits(meta, 0)
        ints[2 * i + 1] = digits(meta, 2)
        tile_copies(i, "start")
    for i in range(n):
        for g in range(groups):
            tmpl[i, g] = packed[i][:taps, g * LANES : (g + 1) * LANES].astype(jnp.float32)
    total[...] = jnp.zeros_like(total)
    wide = lax.broadcasted_iota(jnp.int32, (samples, LANES), 1)

    def item(i, g):
        off, cnt = ints[2 * i], ints[2 * i + 1]
        row = chan * width + g * LANES
        first = off + row

        @pl.when(row < cnt)
        def _():
            def turned(half):
                local = first - half * channels + 2 * width
                turn = local & (LANES - 1)
                slot = half * tiles + g
                low = slots[i, slot].astype(jnp.float32)
                high = slots[i, slot + 1].astype(jnp.float32)
                return pltpu.roll(jnp.where(wide < turn, high, low), (LANES - turn) & (LANES - 1), 1)

            split = channels - first
            rows_f[:samples, :] = turned(jnp.where(split > 0, 0, 1))

            @pl.when((split > 0) & (split < LANES))
            def _():
                rows_f[:samples, :] = jnp.where(wide < split, rows_f[:samples, :], turned(1))

            level = [rows_f[8 * m : 8 * m + 8, :] for m in range(steps + blocks)]
            level = [v * v for v in level]
            span = 1
            while span < steps:
                level = [level[m] + level[m + span] for m in range(len(level) - span)]
                span *= 2
            for m in range(blocks + 1):
                sums[8 * m : 8 * m + 8, :] = level[m]

            def conv(q, acc):
                held = [rows_f[pl.ds(8 * m + q, 8), :] for m in range(steps + blocks - 1)]
                acc, window = list(acc[:blocks]), list(acc[blocks:])
                for b in range(blocks):
                    window[b] = window[b] + sums[pl.ds(8 * b + q, 8), :]
                for a in range(steps):
                    tap = jnp.broadcast_to(tmpl[i, g, pl.ds(8 * a + q, 1), :], (8, LANES))
                    for b in range(blocks):
                        acc[b] = acc[b] + tap * held[a + b]
                return tuple(acc) + tuple(window)

            zero = jnp.zeros((8, LANES), jnp.float32)
            out = lax.fori_loop(0, 8, conv, (zero,) * (2 * blocks))
            acc, window = out[:blocks], out[blocks:]
            energy = jnp.zeros((8, LANES), jnp.float32)
            for a in range(steps):
                t = tmpl[i, g, 8 * a : 8 * a + 8, :]
                energy = energy + t * t
            energy = jnp.sum(energy, axis=0, keepdims=True)
            ratio = jnp.full((1, LANES), taps, jnp.float32) / cnt.astype(jnp.float32)
            gain = lax.rsqrt(energy / taps + 1e-06) * jnp.sqrt(ratio) * (1.0 / taps)
            gain = jnp.where(lane_row + row < cnt, gain, 0.0)
            gain = jnp.broadcast_to(gain, (8, LANES))
            for b in range(blocks):
                scale = lax.rsqrt(window[b] / taps + 1e-06)
                total[i, 8 * b : 8 * b + 8, :] += acc[b] * scale * gain

    rows_f[(samples // 8) * 8 :, :] = jnp.zeros_like(rows_f[(samples // 8) * 8 :, :])
    for i in range(n):
        tile_copies(i, "wait")

    def step(index, _):
        item(index // groups, index % groups)
        return 0

    lax.fori_loop(0, n * groups, step, 0)
    ones = jnp.ones((8, LANES), jnp.float32)
    sub = lax.broadcasted_iota(jnp.int32, prev.shape, 0)
    result = prev[...]
    blk = lax.axis_index("blk")
    for i in range(n):
        row = lax.dot_general(
            ones, total[i], (((1,), (1,)), ((), ())),
            precision=lax.Precision.HIGHEST, preferred_element_type=jnp.float32,
        )[:1]
        at = places[i][0] if places[i][1] else blk ^ places[i][0]
        result = result + jnp.where(sub == at, row, 0.0)
    if not last:
        outs[0][...] = result
        return
    half = shifts // 2
    left, right = result[:, :half], result[:, half:]
    outs[0][...] = jnp.where(chan == 0, left, right)
    outs[1][...] = jnp.where(chan == 0, right, left)


def score(records, prev, packed, places, taps, shifts, last):
    n = len(packed)
    mine, theirs = records
    samples, channels = mine.shape
    rows = packed[0].shape[1]
    groups = rows // LANES
    k = prev.shape[0]
    vmem = pl.BlockSpec(memory_space=pltpu.VMEM)
    anywhere = pl.BlockSpec(memory_space=pl.ANY)
    tail = pl.BlockSpec((samples, LANES), lambda _: (0, (channels - 1) // LANES))
    if last:
        out = jax.ShapeDtypeStruct((k, shifts // 2), jnp.float32)
        out_shape, out_specs = (out, out), (vmem, vmem)
    else:
        out_shape, out_specs = jax.ShapeDtypeStruct((k, shifts), jnp.float32), vmem
    return pl.pallas_call(
        functools.partial(score_kernel, taps, shifts, places, last),
        out_shape=out_shape,
        grid=(1,),
        in_specs=[anywhere, anywhere, tail, tail, vmem] + [vmem] * n,
        out_specs=out_specs,
        scratch_shapes=[
            pltpu.VMEM((n, groups, taps, LANES), jnp.float32),
            pltpu.SMEM((2 * n,), jnp.int32),
            pltpu.VMEM((n, 2 * (groups + 1), samples, LANES), mine.dtype),
            pltpu.VMEM((-(-samples // 8) * 8, LANES), jnp.float32),
            pltpu.VMEM((shifts + 8, LANES), jnp.float32),
            pltpu.VMEM((n, shifts, LANES), jnp.float32),
            pltpu.SemaphoreType.DMA((n, 2 * (groups + 1))),
        ],
        compiler_params=pltpu.CompilerParams(vmem_limit_bytes=32 * 2**20),
        cost_estimate=pl.CostEstimate(
            flops=2 * n * rows * taps * shifts, bytes_accessed=n * rows * samples * 4, transcendentals=0
        ),
        name="score",
    )(mine, theirs, mine, theirs, prev, *packed)


def exchange(value, axis, size, mask):
    return lax.ppermute(value, axis, [(i, i ^ mask) for i in range(size)])


def on_device(mesh_shape, record, templates, offsets, counts):
    blk = mesh_shape["blk"]
    taps = templates.shape[2]
    shifts = record.shape[2] - taps + 1
    mine = jnp.transpose(record[0])
    theirs = exchange(mine, "chan", 2, 1)
    records = (mine, theirs)
    packed = pack(templates[0], offsets, counts)
    if blk == CHUNK:
        held = {0: packed}
        for mask in (4, 6, 2, 1, 3):
            held[mask] = exchange(packed, "blk", blk, mask)
        rows = jnp.zeros((blk, shifts), jnp.float32)
        first = (0, 2, 1, 3)
        rows = score(
            records, rows, [held[m] for m in first], [(m, False) for m in first], taps, shifts, False
        )
        for mask in (4, 6):
            held[mask + 1] = exchange(held[mask], "blk", blk, 1)
        rows = score(
            records, rows, [held[4], held[6]], [(4, False), (6, False)], taps, shifts, False
        )
        keep, send = score(
            records, rows, [held[5], held[7]], [(5, False), (7, False)], taps, shifts, True
        )
    else:
        every = lax.all_gather(packed, "blk", axis=0, tiled=False)
        keeps, sends = [], []
        for at in range(0, blk, CHUNK):
            size = min(CHUNK, blk - at)
            keep, send = score(
                records, jnp.zeros((size, shifts), jnp.float32), [every[at + i] for i in range(size)],
                [(i, True) for i in range(size)], taps, shifts, True,
            )
            keeps.append(keep)
            sends.append(send)
        keep, send = jnp.concatenate(keeps, axis=0), jnp.concatenate(sends, axis=0)
    return (keep + exchange(send, "chan", 2, 1))[None]


def solution(mesh):
    in_specs = (P(("grp", "blk"), "chan", None), P("blk", "chan", None), P("blk"), P("blk"))
    out_specs = P(("grp", "blk"), None, "chan")
    return jax.shard_map(
        functools.partial(on_device, dict(mesh.shape)),
        mesh=mesh, in_specs=in_specs, out_specs=out_specs, check_vma=False,
    )
```

```python
import functools

import jax
import jax.numpy as jnp
from jax import lax
from jax.experimental import pallas as pl
from jax.experimental.pallas import tpu as pltpu
from jax.sharding import PartitionSpec as P

LANES = 128
META = 16
CHUNK = 8


def pack_kernel(off_ref, cnt_ref, tmpl_ref, out_ref):
    rows, taps = tmpl_ref.shape
    out_ref[:taps, :] = jnp.transpose(tmpl_ref[...].astype(jnp.float32)).astype(out_ref.dtype)
    lane = lax.broadcasted_iota(jnp.int32, (META, rows), 1)
    off, cnt = off_ref[0], cnt_ref[0]
    level = lax.broadcasted_iota(jnp.int32, (META, rows), 0)
    value = jnp.where(lane == 0, off, cnt)
    meta = jnp.where(level == 0, value >> 8, value & 255)
    out_ref[taps:, :] = meta.astype(jnp.float32).astype(out_ref.dtype)


def pack(templates, offsets, counts):
    rows, taps = templates.shape
    return pl.pallas_call(
        pack_kernel,
        out_shape=jax.ShapeDtypeStruct((taps + META, rows), templates.dtype),
        in_specs=[
            pl.BlockSpec(memory_space=pltpu.SMEM),
            pl.BlockSpec(memory_space=pltpu.SMEM),
            pl.BlockSpec(memory_space=pltpu.VMEM),
        ],
        out_specs=pl.BlockSpec(memory_space=pltpu.VMEM),
        name="pack",
    )(offsets, counts, templates)


def score_kernel(taps, shifts, places, *refs):
    n = len(places)
    mine, theirs = refs[:2]
    packed = refs[2 : 2 + n]
    keep_ref, send_ref, tmpl, pair, gains, ints_v, ints, tails, rows_f, diff_f, sums, total, sem = refs[2 + n :]
    samples, channels = mine.shape
    width = packed[0].shape[1]
    groups = width // LANES
    whole_tiles = channels // LANES
    rest = channels - whole_tiles * LANES
    chan = lax.axis_index("chan")
    blocks = shifts // 8
    steps = taps // 8
    lane_row = lax.broadcasted_iota(jnp.int32, (1, LANES), 1)

    for i in range(n):
        meta = packed[i][taps:, :LANES].astype(jnp.float32)
        ints_v[i : i + 1, :] = (meta[:1] * 256.0 + meta[1:2]).astype(jnp.int32)
    to_scalars = pltpu.make_async_copy(ints_v, ints, sem)
    to_scalars.start()
    for i in range(n):
        for g in range(groups):
            block = packed[i][:taps, g * LANES : (g + 1) * LANES].astype(jnp.float32)
            tmpl[i * groups + g, :taps, :] = block
            tiles = [block[8 * a : 8 * a + 8] for a in range(steps)]
            energy = jnp.zeros((8, LANES), jnp.float32)
            for a in range(0, steps, 2):
                pair[i * groups + g, 4 * a : 4 * a + 8, :] = tiles[a] + tiles[a + 1]
                energy = energy + (tiles[a] * tiles[a] + tiles[a + 1] * tiles[a + 1])
            gains[i * groups + g : i * groups + g + 1, :] = jnp.sum(energy, axis=0, keepdims=True)
    if rest:
        tails[0, :, :rest] = mine[:, whole_tiles * LANES :]
        tails[1, :, :rest] = theirs[:, whole_tiles * LANES :]
    rows_f[(samples // 8) * 8 :, :] = jnp.zeros_like(rows_f[(samples // 8) * 8 :, :])
    to_scalars.wait()
    for i in range(n):
        count = jnp.full((1, LANES), ints[i, 1], jnp.int32)
        ratio = jnp.sqrt(taps / count.astype(jnp.float32)) * (1.0 / taps)
        for g in range(groups):
            at = i * groups + g
            gain = lax.rsqrt(gains[at : at + 1, :] / taps + 1e-06) * ratio
            gains[at : at + 1, :] = jnp.where(lane_row + (chan * width + g * LANES) < count, gain, 0.0)

    wide = lax.broadcasted_iota(jnp.int32, (samples, LANES), 1)

    def turned(low, high, turn):
        mixed = jnp.where(wide < turn, high.astype(jnp.float32), low.astype(jnp.float32))
        return pltpu.roll(mixed, (LANES - turn) & (LANES - 1), 1)

    def item(index, _):
        i, g = index // groups, index % groups
        first = ints[i, 0] + chan * width + g * LANES
        split = channels - first
        half = jnp.where(split > 0, 0, 1)
        local = first - half * channels
        tile = local >> 7
        fast = ((split >= LANES) | (split <= 0)) & (tile + 1 < whole_tiles)

        for source, here in ((mine, half == chan), (theirs, half != chan)):

            @pl.when(fast & here)
            def _():
                at = pl.multiple_of(tile * LANES, LANES)
                rows_f[:samples, :] = turned(
                    source[:, pl.ds(at, LANES)], source[:, pl.ds(at + LANES, LANES)], local & (LANES - 1)
                )

        @pl.when(jnp.logical_not(fast))
        def _():
            sides = []
            for side in range(2):
                begin = first - side * channels
                turn = begin & (LANES - 1)
                found = []
                for m in range(2):
                    want = (begin >> 7) + m
                    at = pl.multiple_of(jnp.clip(want, 0, whole_tiles - 1) * LANES, LANES)
                    value = jnp.where(
                        chan == side,
                        mine[:, pl.ds(at, LANES)].astype(jnp.float32),
                        theirs[:, pl.ds(at, LANES)].astype(jnp.float32),
                    )
                    if rest:
                        tail = tails[jnp.where(chan == side, 0, 1)].astype(jnp.float32)
                        value = jnp.where(want >= whole_tiles, tail, value)
                    found.append(value)
                sides.append(turned(found[0], found[1], turn))
            rows_f[:samples, :] = jnp.where(wide < split, sides[0], sides[1])

        held = [rows_f[8 * m : 8 * m + 8, :] for m in range(steps + blocks)]
        for m in range(steps + blocks - 1):
            diff_f[8 * m : 8 * m + 8, :] = held[m] - held[m + 1]
        level = [v * v for v in held]
        span = 1
        while span < steps:
            level = [level[m] + level[m + span] for m in range(len(level) - span)]
            span *= 2
        for m in range(blocks + 1):
            sums[8 * m : 8 * m + 8, :] = level[m]

        half_blocks, half_steps = blocks // 2, steps // 2
        reach = half_blocks + half_steps - 1

        def conv(twice, carry):
            lists = [list(part) for part in carry]
            one, two, three, window = lists
            for extra in range(2):
                q = 2 * twice + extra
                for b in range(blocks):
                    window[b] = window[b] + sums[pl.ds(8 * b + q, 8), :]
                even = [diff_f[pl.ds(16 * m + q, 8), :] for m in range(reach)]
                odd = [rows_f[pl.ds(16 * m + 8 + q, 8), :] for m in range(reach)]
                next_even = [diff_f[pl.ds(16 * m + 8 + q, 8), :] for m in range(reach)]
                for a in range(half_steps):
                    t0 = tmpl[index, pl.ds(16 * a + q, 8, stride=0), :]
                    t1 = tmpl[index, pl.ds(16 * a + 8 + q, 8, stride=0), :]
                    both = pair[index, pl.ds(8 * a + q, 8, stride=0), :]
                    for b in range(half_blocks):
                        one[b] = one[b] + t0 * even[a + b]
                        two[b] = two[b] + both * odd[a + b]
                        three[b] = three[b] + t1 * next_even[a + b]
            return tuple(tuple(part) for part in lists)

        zero = jnp.zeros((8, LANES), jnp.float32)
        start = ((zero,) * half_blocks,) * 3 + ((zero,) * blocks,)
        one, two, three, window = lax.fori_loop(0, 4, conv, start)
        gain = gains[pl.ds(index, 8, stride=0), :]
        for b in range(blocks):
            product = one[b // 2] + two[b // 2] if b % 2 == 0 else two[b // 2] - three[b // 2]
            value = product * lax.rsqrt(window[b] / taps + 1e-06) * gain
            at = pl.multiple_of(i * shifts + 8 * b, 8)
            total[pl.ds(at, 8), :] = jnp.where(g == 0, value, total[pl.ds(at, 8), :] + value)
        return 0

    lax.fori_loop(0, n * groups, item, 0)
    stacked = lax.dot_general(
        jnp.ones((8, LANES), jnp.float32), total[...], (((1,), (1,)), ((), ())),
        precision=lax.Precision.HIGHEST, preferred_element_type=jnp.float32,
    )
    sub = lax.broadcasted_iota(jnp.int32, (n, shifts), 0)
    blk = lax.axis_index("blk")
    result = jnp.zeros((n, shifts), jnp.float32)
    for i in range(n):
        at = places[i][0] if places[i][1] else blk ^ places[i][0]
        result = jnp.where(sub == at, stacked[:1, i * shifts : (i + 1) * shifts], result)
    left, right = result[:, : shifts // 2], result[:, shifts // 2 :]
    keep_ref[...] = jnp.where(chan == 0, left, right)
    send_ref[...] = jnp.where(chan == 0, right, left)


def score(records, packed, places, taps, shifts):
    n = len(packed)
    samples, channels = records[0].shape
    width = packed[0].shape[1]
    groups = width // LANES
    items = n * groups
    padded = -(-samples // 8) * 8
    vmem = pl.BlockSpec(memory_space=pltpu.VMEM)
    out = jax.ShapeDtypeStruct((n, shifts // 2), jnp.float32)
    return pl.pallas_call(
        functools.partial(score_kernel, taps, shifts, places),
        out_shape=(out, out),
        in_specs=[vmem] * (2 + n),
        out_specs=(vmem, vmem),
        scratch_shapes=[
            pltpu.VMEM((items, taps + 8, LANES), jnp.float32),
            pltpu.VMEM((items, taps // 2 + 8, LANES), jnp.float32),
            pltpu.VMEM((-(-items // 8) * 8 + 8, LANES), jnp.float32),
            pltpu.VMEM((n, LANES), jnp.int32),
            pltpu.SMEM((n, LANES), jnp.int32),
            pltpu.VMEM((2, samples, LANES), records[0].dtype),
            pltpu.VMEM((padded, LANES), jnp.float32),
            pltpu.VMEM((padded, LANES), jnp.float32),
            pltpu.VMEM((shifts + 8, LANES), jnp.float32),
            pltpu.VMEM((n * shifts, LANES), jnp.float32),
            pltpu.SemaphoreType.DMA,
        ],
        compiler_params=pltpu.CompilerParams(vmem_limit_bytes=32 * 2**20),
        cost_estimate=pl.CostEstimate(
            flops=2 * n * width * taps * shifts, bytes_accessed=n * width * samples * 4, transcendentals=0
        ),
        name="score",
    )(*records, *packed)


def exchange(value, axis, size, mask):
    return lax.ppermute(value, axis, [(i, i ^ mask) for i in range(size)])


def on_device(mesh_shape, record, templates, offsets, counts):
    blk = mesh_shape["blk"]
    taps = templates.shape[2]
    shifts = record.shape[2] - taps + 1
    packed = pack(templates[0], offsets, counts)
    mine = jnp.transpose(record[0])
    packed, mine = lax.optimization_barrier((packed, mine))
    if blk == CHUNK:
        held = {0: packed}
        for mask in (4, 2, 1):
            held[mask] = exchange(packed, "blk", blk, mask)
        theirs = exchange(mine, "chan", 2, 1)
        held[6] = exchange(held[4], "blk", blk, 2)
        for mask in (4, 2, 6):
            held[mask + 1] = exchange(held[mask], "blk", blk, 1)
        keep, send = score(
            (mine, theirs), [held[m] for m in range(blk)], [(m, False) for m in range(blk)], taps, shifts
        )
    else:
        theirs = exchange(mine, "chan", 2, 1)
        every = lax.all_gather(packed, "blk", axis=0, tiled=False)
        keeps, sends = [], []
        for at in range(0, blk, CHUNK):
            size = min(CHUNK, blk - at)
            keep, send = score(
                (mine, theirs), [every[at + i] for i in range(size)],
                [(i, True) for i in range(size)], taps, shifts,
            )
            keeps.append(keep)
            sends.append(send)
        keep, send = jnp.concatenate(keeps, axis=0), jnp.concatenate(sends, axis=0)
    return (keep + exchange(send, "chan", 2, 1))[None]


def solution(mesh):
    in_specs = (P(("grp", "blk"), "chan", None), P("blk", "chan", None), P("blk"), P("blk"))
    out_specs = P(("grp", "blk"), None, "chan")
    return jax.shard_map(
        functools.partial(on_device, dict(mesh.shape)),
        mesh=mesh, in_specs=in_specs, out_specs=out_specs, check_vma=False,
    )
```

```python
import functools

import jax
import jax.numpy as jnp
from jax import lax
from jax.experimental import pallas as pl
from jax.experimental.pallas import tpu as pltpu
from jax.sharding import PartitionSpec as P

LANES = 128
META = 16
CHUNK = 8


def pack_kernel(off_ref, cnt_ref, tmpl_ref, out_ref, own_ref):
    rows, taps = tmpl_ref.shape
    turned = jnp.transpose(tmpl_ref[...].astype(jnp.float32)).astype(out_ref.dtype)
    out_ref[:taps, :] = turned
    own_ref[:taps, :] = turned
    lane = lax.broadcasted_iota(jnp.int32, (META, rows), 1)
    off, cnt = off_ref[0], cnt_ref[0]
    level = lax.broadcasted_iota(jnp.int32, (META, rows), 0)
    value = jnp.where(lane == 0, off, cnt)
    meta = jnp.where(level == 0, value >> 8, value & 255)
    meta = meta.astype(jnp.float32).astype(out_ref.dtype)
    out_ref[taps:, :] = meta
    own_ref[taps:, :] = meta


def pack(templates, offsets, counts):
    rows, taps = templates.shape
    return pl.pallas_call(
        pack_kernel,
        out_shape=(jax.ShapeDtypeStruct((taps + META, rows), templates.dtype),) * 2,
        in_specs=[
            pl.BlockSpec(memory_space=pltpu.SMEM),
            pl.BlockSpec(memory_space=pltpu.SMEM),
            pl.BlockSpec(memory_space=pltpu.VMEM),
        ],
        out_specs=(pl.BlockSpec(memory_space=pltpu.VMEM),) * 2,
        cost_estimate=pl.CostEstimate(flops=4 * 10**9, bytes_accessed=10**7, transcendentals=0),
        name="pack",
    )(offsets, counts, templates)


def score_kernel(taps, shifts, places, more, last, *refs):
    n = len(places)
    mine, theirs = refs[:2]
    packed = refs[2 : 2 + n]
    at = 2 + n + more
    prev_ref, outs = refs[2 + n : at], refs[at : at + 1 + last]
    tmpl, pair, gains, ints_v, ints, tails, rows_f, diff_f, sums, total, sem = refs[at + 1 + last :]
    samples, channels = mine.shape
    width = packed[0].shape[1]
    groups = width // LANES
    whole_tiles = channels // LANES
    rest = channels - whole_tiles * LANES
    chan = lax.axis_index("chan")
    blocks = shifts // 8
    steps = taps // 8
    lane_row = lax.broadcasted_iota(jnp.int32, (1, LANES), 1)

    for i in range(n):
        meta = packed[i][taps:, :LANES].astype(jnp.float32)
        ints_v[i : i + 1, :] = (meta[:1] * 256.0 + meta[1:2]).astype(jnp.int32)
    to_scalars = pltpu.make_async_copy(ints_v, ints, sem)
    to_scalars.start()
    for i in range(n):
        for g in range(groups):
            block = packed[i][:taps, g * LANES : (g + 1) * LANES].astype(jnp.float32)
            tmpl[i * groups + g, :taps, :] = block
            tiles = [block[8 * a : 8 * a + 8] for a in range(steps)]
            energy = jnp.zeros((8, LANES), jnp.float32)
            for a in range(0, steps, 2):
                pair[i * groups + g, 4 * a : 4 * a + 8, :] = tiles[a] + tiles[a + 1]
                energy = energy + (tiles[a] * tiles[a] + tiles[a + 1] * tiles[a + 1])
            gains[i * groups + g : i * groups + g + 1, :] = jnp.sum(energy, axis=0, keepdims=True)
    if rest:
        tails[0, :, :rest] = mine[:, whole_tiles * LANES :]
        tails[1, :, :rest] = theirs[:, whole_tiles * LANES :]
    rows_f[(samples // 8) * 8 :, :] = jnp.zeros_like(rows_f[(samples // 8) * 8 :, :])
    to_scalars.wait()
    for i in range(n):
        count = jnp.full((1, LANES), ints[i, 1], jnp.int32)
        ratio = jnp.sqrt(taps / count.astype(jnp.float32)) * (1.0 / taps)
        for g in range(groups):
            at = i * groups + g
            gain = lax.rsqrt(gains[at : at + 1, :] / taps + 1e-06) * ratio
            gains[at : at + 1, :] = jnp.where(lane_row + (chan * width + g * LANES) < count, gain, 0.0)

    wide = lax.broadcasted_iota(jnp.int32, (samples, LANES), 1)

    def turned(low, high, turn):
        mixed = jnp.where(wide < turn, high.astype(jnp.float32), low.astype(jnp.float32))
        return pltpu.roll(mixed, (LANES - turn) & (LANES - 1), 1)

    def item(index, _):
        i, g = index // groups, index % groups
        first = ints[i, 0] + chan * width + g * LANES
        split = channels - first
        half = jnp.where(split > 0, 0, 1)
        local = first - half * channels
        tile = local >> 7
        fast = ((split >= LANES) | (split <= 0)) & (tile + 1 < whole_tiles)

        for source, here in ((mine, half == chan), (theirs, half != chan)):

            @pl.when(fast & here)
            def _():
                at = pl.multiple_of(tile * LANES, LANES)
                rows_f[:samples, :] = turned(
                    source[:, pl.ds(at, LANES)], source[:, pl.ds(at + LANES, LANES)], local & (LANES - 1)
                )

        @pl.when(jnp.logical_not(fast))
        def _():
            sides = []
            for side in range(2):
                begin = first - side * channels
                turn = begin & (LANES - 1)
                found = []
                for m in range(2):
                    want = (begin >> 7) + m
                    at = pl.multiple_of(jnp.clip(want, 0, whole_tiles - 1) * LANES, LANES)
                    value = jnp.where(
                        chan == side,
                        mine[:, pl.ds(at, LANES)].astype(jnp.float32),
                        theirs[:, pl.ds(at, LANES)].astype(jnp.float32),
                    )
                    if rest:
                        tail = tails[jnp.where(chan == side, 0, 1)].astype(jnp.float32)
                        value = jnp.where(want >= whole_tiles, tail, value)
                    found.append(value)
                sides.append(turned(found[0], found[1], turn))
            rows_f[:samples, :] = jnp.where(wide < split, sides[0], sides[1])

        held = [rows_f[8 * m : 8 * m + 8, :] for m in range(steps + blocks)]
        for m in range(steps + blocks - 1):
            diff_f[8 * m : 8 * m + 8, :] = held[m] - held[m + 1]
        level = [v * v for v in held]
        span = 1
        while span < steps:
            level = [level[m] + level[m + span] for m in range(len(level) - span)]
            span *= 2
        for m in range(blocks + 1):
            sums[8 * m : 8 * m + 8, :] = level[m]

        half_blocks, half_steps = blocks // 2, steps // 2
        reach = half_blocks + half_steps - 1

        zero = jnp.zeros((8, LANES), jnp.float32)
        one, two, three = ([zero] * half_blocks for _ in range(3))
        window = [zero] * blocks
        origin = index >> 16
        for q in range(8):
            row = origin + q
            for b in range(blocks):
                window[b] = window[b] + sums[pl.ds(8 * b + row, 8), :]
            even = [diff_f[pl.ds(16 * m + row, 8), :] for m in range(reach)]
            odd = [rows_f[pl.ds(16 * m + 8 + row, 8), :] for m in range(reach)]
            next_even = [diff_f[pl.ds(16 * m + 8 + row, 8), :] for m in range(reach)]
            for a in range(half_steps):
                t0 = tmpl[index, pl.ds(16 * a + row, 8, stride=0), :]
                t1 = tmpl[index, pl.ds(16 * a + 8 + row, 8, stride=0), :]
                both = pair[index, pl.ds(8 * a + row, 8, stride=0), :]
                for b in range(half_blocks):
                    one[b] = one[b] + t0 * even[a + b]
                    two[b] = two[b] + both * odd[a + b]
                    three[b] = three[b] + t1 * next_even[a + b]
        gain = gains[pl.ds(index, 8, stride=0), :]
        for b in range(blocks):
            product = one[b // 2] + two[b // 2] if b % 2 == 0 else two[b // 2] - three[b // 2]
            value = product * lax.rsqrt(window[b] / taps + 1e-06) * gain
            at = pl.multiple_of(i * shifts + 8 * b, 8)
            total[pl.ds(at, 8), :] = jnp.where(g == 0, value, total[pl.ds(at, 8), :] + value)
        return 0

    lax.fori_loop(0, n * groups, item, 0)
    rest_f = total[...]
    stacked = jnp.zeros((8, n * shifts), jnp.float32)
    for _ in range(3):
        term = rest_f.astype(jnp.bfloat16)
        rest_f = rest_f - term.astype(jnp.float32)
        stacked = stacked + lax.dot_general(
            jnp.ones((8, LANES), jnp.bfloat16), term, (((1,), (1,)), ((), ())),
            preferred_element_type=jnp.float32,
        )
    result = prev_ref[0][...] if more else jnp.zeros(outs[0].shape[:1] + (shifts,), jnp.float32)
    sub = lax.broadcasted_iota(jnp.int32, result.shape, 0)
    blk = lax.axis_index("blk")
    for i in range(n):
        row = places[i][0] if places[i][1] else blk ^ places[i][0]
        result = jnp.where(sub == row, stacked[:1, i * shifts : (i + 1) * shifts], result)
    if not last:
        outs[0][...] = result
        return
    left, right = result[:, : shifts // 2], result[:, shifts // 2 :]
    outs[0][...] = jnp.where(chan == 0, left, right)
    outs[1][...] = jnp.where(chan == 0, right, left)


def score(records, packed, places, templates, taps, shifts, prev=(), last=True):
    n = len(packed)
    samples, channels = records[0].shape
    width = packed[0].shape[1]
    groups = width // LANES
    items = n * groups
    padded = -(-samples // 8) * 8
    vmem = pl.BlockSpec(memory_space=pltpu.VMEM)
    if last:
        out_shape = (jax.ShapeDtypeStruct((templates, shifts // 2), jnp.float32),) * 2
    else:
        out_shape = (jax.ShapeDtypeStruct((templates, shifts), jnp.float32),)
    return pl.pallas_call(
        functools.partial(score_kernel, taps, shifts, places, len(prev), int(last)),
        out_shape=out_shape,
        in_specs=[vmem] * (2 + n + len(prev)),
        out_specs=(vmem,) * len(out_shape),
        scratch_shapes=[
            pltpu.VMEM((items, taps + 8, LANES), jnp.float32),
            pltpu.VMEM((items, taps // 2 + 8, LANES), jnp.float32),
            pltpu.VMEM((-(-items // 8) * 8 + 8, LANES), jnp.float32),
            pltpu.VMEM((n, LANES), jnp.int32),
            pltpu.SMEM((n, LANES), jnp.int32),
            pltpu.VMEM((2, samples, LANES), records[0].dtype),
            pltpu.VMEM((padded, LANES), jnp.float32),
            pltpu.VMEM((padded, LANES), jnp.float32),
            pltpu.VMEM((shifts + 8, LANES), jnp.float32),
            pltpu.VMEM((n * shifts, LANES), jnp.float32),
            pltpu.SemaphoreType.DMA,
        ],
        compiler_params=pltpu.CompilerParams(vmem_limit_bytes=32 * 2**20),
        cost_estimate=pl.CostEstimate(
            flops=2 * n * width * taps * shifts, bytes_accessed=n * width * samples * 4, transcendentals=0
        ),
        name="score",
    )(*records, *packed, *prev)


def exchange(value, axis, size, mask):
    return lax.ppermute(value, axis, [(i, i ^ mask) for i in range(size)])


def on_device(mesh_shape, record, templates, offsets, counts):
    blk = mesh_shape["blk"]
    taps = templates.shape[2]
    shifts = record.shape[2] - taps + 1
    packed, own = pack(templates[0], offsets, counts)
    mine = jnp.transpose(record[0])
    packed, mine = lax.optimization_barrier((packed, mine))
    if blk == CHUNK:
        held = {0: own}
        for mask in (4, 1, 2):
            held[mask] = exchange(packed, "blk", blk, mask)
        theirs = exchange(mine, "chan", 2, 1)
        held[3] = exchange(held[1], "blk", blk, 2)
        held[6] = exchange(held[4], "blk", blk, 2)
        held[5] = exchange(held[4], "blk", blk, 1)
        held[7] = exchange(held[6], "blk", blk, 1)
        rows = ()
        for masks, last in (((0, 1, 2, 4), False), ((3, 5, 6, 7), True)):
            rows = score(
                (mine, theirs), [held[m] for m in masks], [(m, False) for m in masks],
                blk, taps, shifts, rows, last,
            )
        keep, send = rows
    else:
        theirs = exchange(mine, "chan", 2, 1)
        every = lax.all_gather(packed, "blk", axis=0, tiled=False)
        keeps, sends = [], []
        for at in range(0, blk, CHUNK):
            size = min(CHUNK, blk - at)
            keep, send = score(
                (mine, theirs), [every[at + i] for i in range(size)],
                [(i, True) for i in range(size)], size, taps, shifts,
            )
            keeps.append(keep)
            sends.append(send)
        keep, send = jnp.concatenate(keeps, axis=0), jnp.concatenate(sends, axis=0)
    return (keep + exchange(send, "chan", 2, 1))[None]


def solution(mesh):
    in_specs = (P(("grp", "blk"), "chan", None), P("blk", "chan", None), P("blk"), P("blk"))
    out_specs = P(("grp", "blk"), None, "chan")
    return jax.shard_map(
        functools.partial(on_device, dict(mesh.shape)),
        mesh=mesh, in_specs=in_specs, out_specs=out_specs, check_vma=False,
    )
```

```python
import functools

import jax
import jax.numpy as jnp
from jax import lax
from jax.experimental import pallas as pl
from jax.experimental.pallas import tpu as pltpu
from jax.sharding import PartitionSpec as P

LANES = 128
META = 16
CHUNK = 8
PITCH = 9


def pack_kernel(off_ref, cnt_ref, tmpl_ref, out_ref, own_ref):
    rows, taps = tmpl_ref.shape
    turned = jnp.transpose(tmpl_ref[...].astype(jnp.float32)).astype(out_ref.dtype)
    out_ref[:taps, :] = turned
    own_ref[:taps, :] = turned
    lane = lax.broadcasted_iota(jnp.int32, (META, rows), 1)
    off, cnt = off_ref[0], cnt_ref[0]
    level = lax.broadcasted_iota(jnp.int32, (META, rows), 0)
    value = jnp.where(lane == 0, off, cnt)
    meta = jnp.where(level == 0, value >> 8, value & 255)
    meta = meta.astype(jnp.float32).astype(out_ref.dtype)
    out_ref[taps:, :] = meta
    own_ref[taps:, :] = meta


def pack(templates, offsets, counts):
    rows, taps = templates.shape
    return pl.pallas_call(
        pack_kernel,
        out_shape=(jax.ShapeDtypeStruct((taps + META, rows), templates.dtype),) * 2,
        in_specs=[
            pl.BlockSpec(memory_space=pltpu.SMEM),
            pl.BlockSpec(memory_space=pltpu.SMEM),
            pl.BlockSpec(memory_space=pltpu.VMEM),
        ],
        out_specs=(pl.BlockSpec(memory_space=pltpu.VMEM),) * 2,
        cost_estimate=pl.CostEstimate(flops=4 * 10**9, bytes_accessed=10**7, transcendentals=0),
        compiler_params=pltpu.CompilerParams(vmem_limit_bytes=4 * 2**20),
        name="pack",
    )(offsets, counts, templates)


def score_kernel(taps, shifts, places, more, last, *refs):
    n = len(places)
    mine, theirs = refs[:2]
    packed = refs[2 : 2 + n]
    at = 2 + n + more
    prev_ref, outs = refs[2 + n : at], refs[at : at + 1 + last]
    tmpl, gains, ints_v, ints, tails, rows_f, pitched, sums, total, sem = refs[at + 1 + last :]
    samples, channels = mine.shape
    width = packed[0].shape[1]
    groups = width // LANES
    whole_tiles = channels // LANES
    rest = channels - whole_tiles * LANES
    chan = lax.axis_index("chan")
    blocks = shifts // 8
    steps = taps // 8
    lane_row = lax.broadcasted_iota(jnp.int32, (1, LANES), 1)

    for i in range(n):
        meta = packed[i][taps:, :LANES].astype(jnp.float32)
        ints_v[i : i + 1, :] = (meta[:1] * 256.0 + meta[1:2]).astype(jnp.int32)
    to_scalars = pltpu.make_async_copy(ints_v, ints, sem)
    to_scalars.start()
    for i in range(n):
        for g in range(groups):
            block = packed[i][:taps, g * LANES : (g + 1) * LANES].astype(jnp.float32)
            tmpl[i * groups + g, :taps, :] = block
            tiles = [block[8 * a : 8 * a + 8] for a in range(steps)]
            energy = jnp.zeros((8, LANES), jnp.float32)
            for a in range(0, steps, 2):
                energy = energy + (tiles[a] * tiles[a] + tiles[a + 1] * tiles[a + 1])
            gains[i * groups + g : i * groups + g + 1, :] = jnp.sum(energy, axis=0, keepdims=True)
    if rest:
        tails[0, :, :rest] = mine[:, whole_tiles * LANES :]
        tails[1, :, :rest] = theirs[:, whole_tiles * LANES :]
    rows_f[(samples // 8) * 8 :, :] = jnp.zeros_like(rows_f[(samples // 8) * 8 :, :])
    to_scalars.wait()
    for i in range(n):
        count = jnp.full((1, LANES), ints[i, 1], jnp.int32)
        ratio = jnp.sqrt(taps / count.astype(jnp.float32)) * (1.0 / taps)
        for g in range(groups):
            at = i * groups + g
            gain = lax.rsqrt(gains[at : at + 1, :] / taps + 1e-06) * ratio
            gains[at : at + 1, :] = jnp.where(lane_row + (chan * width + g * LANES) < count, gain, 0.0)

    wide = lax.broadcasted_iota(jnp.int32, (samples, LANES), 1)

    def turned(low, high, turn):
        mixed = jnp.where(wide < turn, high.astype(jnp.float32), low.astype(jnp.float32))
        return pltpu.roll(mixed, (LANES - turn) & (LANES - 1), 1)

    def item(index, _):
        i, g = index // groups, index % groups
        first = ints[i, 0] + chan * width + g * LANES
        split = channels - first
        half = jnp.where(split > 0, 0, 1)
        local = first - half * channels
        tile = local >> 7
        fast = ((split >= LANES) | (split <= 0)) & (tile + 1 < whole_tiles)

        for source, here in ((mine, half == chan), (theirs, half != chan)):

            @pl.when(fast & here)
            def _():
                at = pl.multiple_of(tile * LANES, LANES)
                rows_f[:samples, :] = turned(
                    source[:, pl.ds(at, LANES)], source[:, pl.ds(at + LANES, LANES)], local & (LANES - 1)
                )

        @pl.when(jnp.logical_not(fast))
        def _():
            sides = []
            for side in range(2):
                begin = first - side * channels
                turn = begin & (LANES - 1)
                found = []
                for m in range(2):
                    want = (begin >> 7) + m
                    at = pl.multiple_of(jnp.clip(want, 0, whole_tiles - 1) * LANES, LANES)
                    value = jnp.where(
                        chan == side,
                        mine[:, pl.ds(at, LANES)].astype(jnp.float32),
                        theirs[:, pl.ds(at, LANES)].astype(jnp.float32),
                    )
                    if rest:
                        tail = tails[jnp.where(chan == side, 0, 1)].astype(jnp.float32)
                        value = jnp.where(want >= whole_tiles, tail, value)
                    found.append(value)
                sides.append(turned(found[0], found[1], turn))
            rows_f[:samples, :] = jnp.where(wide < split, sides[0], sides[1])

        origin = index >> 16
        held = [rows_f[8 * m : 8 * m + 8, :] for m in range(steps + blocks)]
        for m in range(steps + blocks):
            pitched[pl.ds(origin + PITCH * m, 8), :] = held[m]

        level = [v * v for v in held]
        span = 1
        while span < steps:
            level = [level[m] + level[m + span] for m in range(len(level) - span)]
            span *= 2
        for m in range(blocks + 1):
            sums[pl.ds(origin + PITCH * m, 8), :] = level[m]

        def spread(ref, m):
            return ref[pl.ds(m + m // 8, 8, stride=PITCH), :]

        near = [spread(sums, m) for m in range(15)]
        before, after = [near[7]], [near[8]]
        for m in range(1, 8):
            before.append(before[-1] + near[7 - m])
        for m in range(1, 7):
            after.append(after[-1] + near[8 + m])
        window = [before[7]] + [before[7 - b] + after[b - 1] for b in range(1, 8)]

        zero = jnp.zeros((8, LANES), jnp.float32)
        one, two, three = ([zero] * 4 for _ in range(3))
        data = [spread(pitched, m) for m in range(7)]
        even = [data[2 * m] - data[2 * m + 1] for m in range(3)]
        odd = [data[2 * m + 1] for m in range(3)]
        next_even = [data[2 * m + 1] - data[2 * m + 2] for m in range(3)]
        current = data[6]
        for a in range(taps // 2):
            middle, following = spread(pitched, 2 * a + 7), spread(pitched, 2 * a + 8)
            even.append(current - middle)
            odd.append(middle)
            next_even.append(middle - following)
            current = following
            t0 = tmpl[index, pl.ds(2 * a, 8, stride=0), :]
            t1 = tmpl[index, pl.ds(2 * a + 1, 8, stride=0), :]
            both = t0 + t1
            for b in range(4):
                one[b] = one[b] + t0 * even[a + b]
                two[b] = two[b] + both * odd[a + b]
                three[b] = three[b] + t1 * next_even[a + b]
        gain = gains[pl.ds(index, 8, stride=0), :]
        for b in range(8):
            product = one[b // 2] + two[b // 2] if b % 2 == 0 else two[b // 2] - three[b // 2]
            value = product * lax.rsqrt(window[b] / taps + 1e-06) * gain
            total[pl.ds((i * groups + g) * shifts + b, 8, stride=8), :] = value
        return 0

    lax.fori_loop(0, n * groups, item, 0)
    rest_f = jnp.concatenate(
        [
            sum(total[(i * groups + g) * shifts : (i * groups + g + 1) * shifts, :] for g in range(groups))
            for i in range(n)
        ],
        axis=0,
    )
    stacked = jnp.zeros((8, n * shifts), jnp.float32)
    for _ in range(3):
        term = rest_f.astype(jnp.bfloat16)
        rest_f = rest_f - term.astype(jnp.float32)
        stacked = stacked + lax.dot_general(
            jnp.ones((8, LANES), jnp.bfloat16), term, (((1,), (1,)), ((), ())),
            preferred_element_type=jnp.float32,
        )
    result = prev_ref[0][...] if more else jnp.zeros(outs[0].shape[:1] + (shifts,), jnp.float32)
    sub = lax.broadcasted_iota(jnp.int32, result.shape, 0)
    blk = lax.axis_index("blk")
    for i in range(n):
        row = places[i][0] if places[i][1] else blk ^ places[i][0]
        result = jnp.where(sub == row, stacked[:1, i * shifts : (i + 1) * shifts], result)
    if not last:
        outs[0][...] = result
        return
    left, right = result[:, : shifts // 2], result[:, shifts // 2 :]
    outs[0][...] = jnp.where(chan == 0, left, right)
    outs[1][...] = jnp.where(chan == 0, right, left)


def score(records, packed, places, templates, taps, shifts, prev=(), last=True):
    n = len(packed)
    samples, channels = records[0].shape
    width = packed[0].shape[1]
    groups = width // LANES
    items = n * groups
    padded = -(-samples // 8) * 8
    vmem = pl.BlockSpec(memory_space=pltpu.VMEM)
    if last:
        out_shape = (jax.ShapeDtypeStruct((templates, shifts // 2), jnp.float32),) * 2
    else:
        out_shape = (jax.ShapeDtypeStruct((templates, shifts), jnp.float32),)
    return pl.pallas_call(
        functools.partial(score_kernel, taps, shifts, places, len(prev), int(last)),
        out_shape=out_shape,
        in_specs=[vmem] * (2 + n + len(prev)),
        out_specs=(vmem,) * len(out_shape),
        scratch_shapes=[
            pltpu.VMEM((items, taps + 8, LANES), jnp.float32),
            pltpu.VMEM((-(-items // 8) * 8 + 8, LANES), jnp.float32),
            pltpu.VMEM((n, LANES), jnp.int32),
            pltpu.SMEM((n, LANES), jnp.int32),
            pltpu.VMEM((2, samples, LANES), records[0].dtype),
            pltpu.VMEM((padded, LANES), jnp.float32),
            pltpu.VMEM((padded // 8 * PITCH + 8, LANES), jnp.float32),
            pltpu.VMEM(((shifts // 8 + 2) * PITCH, LANES), jnp.float32),
            pltpu.VMEM((items * shifts + 8, LANES), jnp.float32),
            pltpu.SemaphoreType.DMA,
        ],
        compiler_params=pltpu.CompilerParams(vmem_limit_bytes=32 * 2**20),
        cost_estimate=pl.CostEstimate(
            flops=2 * n * width * taps * shifts, bytes_accessed=n * width * samples * 4, transcendentals=0
        ),
        name="score",
    )(*records, *packed, *prev)


def exchange(value, axis, size, mask):
    return lax.ppermute(value, axis, [(i, i ^ mask) for i in range(size)])


def on_device(mesh_shape, record, templates, offsets, counts):
    blk = mesh_shape["blk"]
    taps = templates.shape[2]
    shifts = record.shape[2] - taps + 1
    packed, own = pack(templates[0], offsets, counts)
    mine = jnp.transpose(record[0])
    packed, mine = lax.optimization_barrier((packed, mine))
    if blk == CHUNK:
        held = {0: own}
        for mask in (4, 1, 2):
            held[mask] = exchange(packed, "blk", blk, mask)
        theirs = exchange(mine, "chan", 2, 1)
        near = lax.optimization_barrier((held[4], held[1], held[2]))
        held[4], held[1], held[2] = near
        held[3] = exchange(held[1], "blk", blk, 2)
        held[6] = exchange(held[4], "blk", blk, 2)
        held[5] = exchange(held[4], "blk", blk, 1)
        held[7] = exchange(held[6], "blk", blk, 1)
        rows = ()
        for masks, last in (((0, 1, 2, 4), False), ((3, 5, 6, 7), True)):
            rows = score(
                (mine, theirs), [held[m] for m in masks], [(m, False) for m in masks],
                blk, taps, shifts, rows, last,
            )
        keep, send = rows
    else:
        theirs = exchange(mine, "chan", 2, 1)
        every = lax.all_gather(packed, "blk", axis=0, tiled=False)
        keeps, sends = [], []
        for at in range(0, blk, CHUNK):
            size = min(CHUNK, blk - at)
            keep, send = score(
                (mine, theirs), [every[at + i] for i in range(size)],
                [(i, True) for i in range(size)], size, taps, shifts,
            )
            keeps.append(keep)
            sends.append(send)
        keep, send = jnp.concatenate(keeps, axis=0), jnp.concatenate(sends, axis=0)
    return (keep + exchange(send, "chan", 2, 1))[None]


def solution(mesh):
    in_specs = (P(("grp", "blk"), "chan", None), P("blk", "chan", None), P("blk"), P("blk"))
    out_specs = P(("grp", "blk"), None, "chan")
    return jax.shard_map(
        functools.partial(on_device, dict(mesh.shape)),
        mesh=mesh, in_specs=in_specs, out_specs=out_specs, check_vma=False,
    )
```

```python
import functools

import jax
import jax.numpy as jnp
import numpy as np
from jax import lax
from jax.experimental import pallas as pl
from jax.experimental.pallas import tpu as pltpu
from jax.sharding import PartitionSpec as P

LANES = 128
META = 16
CHUNK = 8
PITCH = 9


def pack_kernel(off_ref, cnt_ref, tmpl_ref, out_ref, own_ref):
    rows, taps = tmpl_ref.shape
    turned = jnp.transpose(tmpl_ref[...].astype(jnp.float32)).astype(out_ref.dtype)
    out_ref[:taps, :] = turned
    own_ref[:taps, :] = turned
    lane = lax.broadcasted_iota(jnp.int32, (META, rows), 1)
    off, cnt = off_ref[0], cnt_ref[0]
    level = lax.broadcasted_iota(jnp.int32, (META, rows), 0)
    value = jnp.where(lane == 0, off, cnt)
    meta = jnp.where(level == 0, value >> 8, value & 255)
    meta = meta.astype(jnp.float32).astype(out_ref.dtype)
    out_ref[taps:, :] = meta
    own_ref[taps:, :] = meta


def pack(templates, offsets, counts):
    rows, taps = templates.shape
    return pl.pallas_call(
        pack_kernel,
        out_shape=(jax.ShapeDtypeStruct((taps + META, rows), templates.dtype),) * 2,
        in_specs=[
            pl.BlockSpec(memory_space=pltpu.SMEM),
            pl.BlockSpec(memory_space=pltpu.SMEM),
            pl.BlockSpec(memory_space=pltpu.VMEM),
        ],
        out_specs=(pl.BlockSpec(memory_space=pltpu.VMEM),) * 2,
        cost_estimate=pl.CostEstimate(flops=4 * 10**9, bytes_accessed=10**7, transcendentals=0),
        compiler_params=pltpu.CompilerParams(vmem_limit_bytes=4 * 2**20),
        name="pack",
    )(offsets, counts, templates)


def three_terms(value):
    terms = []
    for _ in range(3):
        terms.append(value.astype(jnp.bfloat16))
        value = value - terms[-1].astype(jnp.float32)
    return terms


def fourier_tables(period, shifts):
    bins = -(-(period // 2 + 1) // 8) * 8
    k = np.arange(bins)[:, None]
    used = k <= period // 2
    angle = 2 * np.pi * k * np.arange(period)[None, :] / period
    forward = np.concatenate([np.cos(angle) * used, np.sin(angle) * used], axis=0)
    weight = np.where((k == 0) | (k == period // 2), 1.0, 2.0) / period
    inverse = np.concatenate([forward[:bins] * weight, -forward[bins:] * weight], axis=0)
    return forward.astype(np.float32), inverse[:, :shifts].T.astype(np.float32)


def score_kernel(taps, shifts, places, more, last, *refs):
    n = len(places)
    mine, theirs, forward, inverse = refs[:4]
    packed = refs[4 : 4 + n]
    at = 4 + n + more
    prev_ref, outs = refs[4 + n : at], refs[at : at + 1 + last]
    gains, ints_v, ints, tails, rows_f, rows_b, sums, scales, sem = refs[at + 1 + last :]
    samples, channels = mine.shape
    width = packed[0].shape[1]
    groups = width // LANES
    whole_tiles = channels // LANES
    rest = channels - whole_tiles * LANES
    chan = lax.axis_index("chan")
    blocks = shifts // 8
    steps = taps // 8
    lane_row = lax.broadcasted_iota(jnp.int32, (1, LANES), 1)

    for i in range(n):
        meta = packed[i][taps:, :LANES].astype(jnp.float32)
        ints_v[i : i + 1, :] = (meta[:1] * 256.0 + meta[1:2]).astype(jnp.int32)
    to_scalars = pltpu.make_async_copy(ints_v, ints, sem)
    to_scalars.start()
    for i in range(n):
        for g in range(groups):
            block = packed[i][:taps, g * LANES : (g + 1) * LANES].astype(jnp.float32)
            tiles = [block[8 * a : 8 * a + 8] for a in range(steps)]
            energy = jnp.zeros((8, LANES), jnp.float32)
            for a in range(0, steps, 2):
                energy = energy + (tiles[a] * tiles[a] + tiles[a + 1] * tiles[a + 1])
            gains[i * groups + g : i * groups + g + 1, :] = jnp.sum(energy, axis=0, keepdims=True)
    if rest:
        tails[0, :, :rest] = mine[:, whole_tiles * LANES :]
        tails[1, :, :rest] = theirs[:, whole_tiles * LANES :]
    rows_f[(samples // 8) * 8 :, :] = jnp.zeros_like(rows_f[(samples // 8) * 8 :, :])
    to_scalars.wait()
    for i in range(n):
        count = jnp.full((1, LANES), ints[i, 1], jnp.int32)
        ratio = jnp.sqrt(taps / count.astype(jnp.float32)) * (1.0 / taps)
        for g in range(groups):
            at = i * groups + g
            gain = lax.rsqrt(gains[at : at + 1, :] / taps + 1e-06) * ratio
            gains[at : at + 1, :] = jnp.where(lane_row + (chan * width + g * LANES) < count, gain, 0.0)

    wide = lax.broadcasted_iota(jnp.int32, (samples, LANES), 1)

    def turned(low, high, turn):
        mixed = jnp.where(wide < turn, high.astype(jnp.float32), low.astype(jnp.float32))
        return pltpu.roll(mixed, (LANES - turn) & (LANES - 1), 1)

    def item(index, _):
        i, g = index // groups, index % groups
        first = ints[i, 0] + chan * width + g * LANES
        split = channels - first
        half = jnp.where(split > 0, 0, 1)
        local = first - half * channels
        tile = local >> 7
        fast = ((split >= LANES) | (split <= 0)) & (tile + 1 < whole_tiles)

        for source, here in ((mine, half == chan), (theirs, half != chan)):

            @pl.when(fast & here)
            def _():
                at = pl.multiple_of(tile * LANES, LANES)
                rows_f[:samples, :] = turned(
                    source[:, pl.ds(at, LANES)], source[:, pl.ds(at + LANES, LANES)], local & (LANES - 1)
                )

        @pl.when(jnp.logical_not(fast))
        def _():
            sides = []
            for side in range(2):
                begin = first - side * channels
                turn = begin & (LANES - 1)
                found = []
                for m in range(2):
                    want = (begin >> 7) + m
                    at = pl.multiple_of(jnp.clip(want, 0, whole_tiles - 1) * LANES, LANES)
                    value = jnp.where(
                        chan == side,
                        mine[:, pl.ds(at, LANES)].astype(jnp.float32),
                        theirs[:, pl.ds(at, LANES)].astype(jnp.float32),
                    )
                    if rest:
                        tail = tails[jnp.where(chan == side, 0, 1)].astype(jnp.float32)
                        value = jnp.where(want >= whole_tiles, tail, value)
                    found.append(value)
                sides.append(turned(found[0], found[1], turn))
            rows_f[:samples, :] = jnp.where(wide < split, sides[0], sides[1])

        rows_b[i, :, pl.ds(pl.multiple_of(g * LANES, LANES), LANES)] = rows_f[...].astype(jnp.bfloat16)

        origin = index >> 16
        level = [rows_f[8 * m : 8 * m + 8, :] for m in range(steps + blocks)]
        level = [v * v for v in level]
        span = 1
        while span < steps:
            level = [level[m] + level[m + span] for m in range(len(level) - span)]
            span *= 2
        for m in range(blocks + 1):
            sums[pl.ds(origin + PITCH * m, 8), :] = level[m]
        near = [sums[pl.ds(m + m // 8, 8, stride=PITCH), :] for m in range(15)]
        before, after = [near[7]], [near[8]]
        for m in range(1, 8):
            before.append(before[-1] + near[7 - m])
        for m in range(1, 7):
            after.append(after[-1] + near[8 + m])
        window = [before[7]] + [before[7 - b] + after[b - 1] for b in range(1, 8)]
        gain = gains[pl.ds(index, 8, stride=0), :]
        for b in range(8):
            scale = lax.rsqrt(window[b] / taps + 1e-06) * gain
            scales[pl.ds(index * shifts + b, 8, stride=8), :] = scale
        return 0

    lax.fori_loop(0, n * groups, item, 0)
    def dot(left, right):
        return jnp.dot(left, right, preferred_element_type=jnp.float32)

    bins = forward.shape[0] // 2
    forward_terms = three_terms(forward[...])
    inverse_terms = jnp.concatenate(three_terms(inverse[...]), axis=0)
    totals = []
    for i in range(n):
        spectra = []
        for value, depth in ((rows_b[i], rows_b.shape[1]), (packed[i][:taps, :], taps)):
            terms = [dot(term[:, :depth], value) for term in forward_terms]
            spectra.append(terms[2] + terms[1] + terms[0])
        rec, tmpl = spectra
        rec_c, rec_s, tmpl_c, tmpl_s = rec[:bins], rec[bins:], tmpl[:bins], tmpl[bins:]
        spectrum = jnp.concatenate(
            [rec_c * tmpl_c + rec_s * tmpl_s, rec_c * tmpl_s - rec_s * tmpl_c], axis=0
        )
        products = [
            dot(inverse_terms[: (3 - m) * shifts, :], term)
            for m, term in enumerate(three_terms(spectrum))
        ]
        small = products[0][2 * shifts :] + products[1][shifts:] + products[2]
        lag = small + (products[0][shifts : 2 * shifts] + products[1][:shifts]) + products[0][:shifts]
        totals.append(
            sum(
                lag[:, g * LANES : (g + 1) * LANES]
                * scales[(i * groups + g) * shifts : (i * groups + g + 1) * shifts, :]
                for g in range(groups)
            )
        )

    ones = jnp.ones((8, LANES), jnp.bfloat16)
    stacked = sum(
        lax.dot_general(ones, term, (((1,), (1,)), ((), ())), preferred_element_type=jnp.float32)
        for term in three_terms(jnp.concatenate(totals, axis=0))
    )
    result = prev_ref[0][...] if more else jnp.zeros(outs[0].shape[:1] + (shifts,), jnp.float32)
    sub = lax.broadcasted_iota(jnp.int32, result.shape, 0)
    blk = lax.axis_index("blk")
    for i in range(n):
        row = places[i][0] if places[i][1] else blk ^ places[i][0]
        result = jnp.where(sub == row, stacked[:1, i * shifts : (i + 1) * shifts], result)
    if not last:
        outs[0][...] = result
        return
    left, right = result[:, : shifts // 2], result[:, shifts // 2 :]
    outs[0][...] = jnp.where(chan == 0, left, right)
    outs[1][...] = jnp.where(chan == 0, right, left)


def score(records, tables, packed, places, templates, taps, shifts, prev=(), last=True):
    n = len(packed)
    samples, channels = records[0].shape
    width = packed[0].shape[1]
    groups = width // LANES
    items = n * groups
    padded = tables[0].shape[1]
    vmem = pl.BlockSpec(memory_space=pltpu.VMEM)
    if last:
        out_shape = (jax.ShapeDtypeStruct((templates, shifts // 2), jnp.float32),) * 2
    else:
        out_shape = (jax.ShapeDtypeStruct((templates, shifts), jnp.float32),)
    return pl.pallas_call(
        functools.partial(score_kernel, taps, shifts, places, len(prev), int(last)),
        out_shape=out_shape,
        in_specs=[vmem] * (4 + n + len(prev)),
        out_specs=(vmem,) * len(out_shape),
        scratch_shapes=[
            pltpu.VMEM((-(-items // 8) * 8 + 8, LANES), jnp.float32),
            pltpu.VMEM((n, LANES), jnp.int32),
            pltpu.SMEM((n, LANES), jnp.int32),
            pltpu.VMEM((2, samples, LANES), records[0].dtype),
            pltpu.VMEM((padded, LANES), jnp.float32),
            pltpu.VMEM((n, padded, width), jnp.bfloat16),
            pltpu.VMEM(((shifts // 8 + 2) * PITCH, LANES), jnp.float32),
            pltpu.VMEM((items * shifts + 8, LANES), jnp.float32),
            pltpu.SemaphoreType.DMA,
        ],
        compiler_params=pltpu.CompilerParams(vmem_limit_bytes=32 * 2**20),
        cost_estimate=pl.CostEstimate(
            flops=2 * n * width * taps * shifts, bytes_accessed=n * width * samples * 4, transcendentals=0
        ),
        name="score",
    )(*records, *tables, *packed, *prev)


def exchange(value, axis, size, mask):
    return lax.ppermute(value, axis, [(i, i ^ mask) for i in range(size)])


def on_device(mesh_shape, record, templates, offsets, counts):
    blk = mesh_shape["blk"]
    taps = templates.shape[2]
    shifts = record.shape[2] - taps + 1
    packed, own = pack(templates[0], offsets, counts)
    mine = jnp.transpose(record[0])
    period = -(-record.shape[2] // 64) * 64
    tables = tuple(jnp.asarray(table) for table in fourier_tables(period, shifts))
    if blk == CHUNK:
        held = {0: own}
        for mask in (4, 1, 2):
            held[mask] = exchange(packed, "blk", blk, mask)
        theirs = exchange(mine, "chan", 2, 1)
        near = lax.optimization_barrier((held[4], held[1], held[2]))
        held[4], held[1], held[2] = near
        held[3] = exchange(held[1], "blk", blk, 2)
        held[6] = exchange(held[4], "blk", blk, 2)
        held[5] = exchange(held[4], "blk", blk, 1)
        held[7] = exchange(held[6], "blk", blk, 1)
        rows = ()
        for masks, last in (((0, 1, 2, 4), False), ((3, 5, 6, 7), True)):
            rows = score(
                (mine, theirs), tables, [held[m] for m in masks], [(m, False) for m in masks],
                blk, taps, shifts, rows, last,
            )
        keep, send = rows
    else:
        theirs = exchange(mine, "chan", 2, 1)
        every = lax.all_gather(packed, "blk", axis=0, tiled=False)
        keeps, sends = [], []
        for at in range(0, blk, CHUNK):
            size = min(CHUNK, blk - at)
            keep, send = score(
                (mine, theirs), tables, [every[at + i] for i in range(size)],
                [(i, True) for i in range(size)], size, taps, shifts,
            )
            keeps.append(keep)
            sends.append(send)
        keep, send = jnp.concatenate(keeps, axis=0), jnp.concatenate(sends, axis=0)
    return (keep + exchange(send, "chan", 2, 1))[None]


def solution(mesh):
    in_specs = (P(("grp", "blk"), "chan", None), P("blk", "chan", None), P("blk"), P("blk"))
    out_specs = P(("grp", "blk"), None, "chan")
    return jax.shard_map(
        functools.partial(on_device, dict(mesh.shape)),
        mesh=mesh, in_specs=in_specs, out_specs=out_specs, check_vma=False,
    )
```

```python
import functools

import jax
import jax.numpy as jnp
import numpy as np
from jax import lax
from jax.experimental import pallas as pl
from jax.experimental.pallas import tpu as pltpu
from jax.sharding import PartitionSpec as P

LANES = 128
META = 16
CHUNK = 8
PITCH = 9


def pack_kernel(off_ref, cnt_ref, tmpl_ref, out_ref, own_ref, off_s, cnt_s, tmpl_v, sems):
    rows, taps = tmpl_ref.shape
    copies = [
        pltpu.make_async_copy(source, target, sems.at[at])
        for at, (source, target) in enumerate(((off_ref, off_s), (cnt_ref, cnt_s), (tmpl_ref, tmpl_v)))
    ]
    for copy in copies:
        copy.start()
    for copy in copies:
        copy.wait()
    turned = jnp.transpose(tmpl_v[...].astype(jnp.float32)).astype(out_ref.dtype)
    out_ref[:taps, :] = turned
    own_ref[:taps, :] = turned
    lane = lax.broadcasted_iota(jnp.int32, (META, rows), 1)
    off, cnt = off_s[0], cnt_s[0]
    level = lax.broadcasted_iota(jnp.int32, (META, rows), 0)
    value = jnp.where(lane == 0, off, cnt)
    meta = jnp.where(level == 0, value >> 8, value & 255)
    meta = meta.astype(jnp.float32).astype(out_ref.dtype)
    out_ref[taps:, :] = meta
    own_ref[taps:, :] = meta


def pack(templates, offsets, counts):
    rows, taps = templates.shape
    return pl.pallas_call(
        pack_kernel,
        out_shape=(jax.ShapeDtypeStruct((taps + META, rows), templates.dtype),) * 2,
        in_specs=[pl.BlockSpec(memory_space=pl.ANY)] * 3,
        scratch_shapes=[
            pltpu.SMEM((1,), jnp.int32),
            pltpu.SMEM((1,), jnp.int32),
            pltpu.VMEM((rows, taps), templates.dtype),
            pltpu.SemaphoreType.DMA((3,)),
        ],
        out_specs=(pl.BlockSpec(memory_space=pltpu.VMEM),) * 2,
        cost_estimate=pl.CostEstimate(flops=4 * 10**9, bytes_accessed=10**7, transcendentals=0),
        compiler_params=pltpu.CompilerParams(vmem_limit_bytes=4 * 2**20),
        name="pack",
    )(offsets, counts, templates)


def three_terms(value):
    terms = []
    for _ in range(3):
        terms.append(value.astype(jnp.bfloat16))
        value = value - terms[-1].astype(jnp.float32)
    return terms


def fourier_tables(period, shifts):
    bins = -(-(period // 2 + 1) // 8) * 8
    k = np.arange(bins)[:, None]
    used = k <= period // 2
    angle = 2 * np.pi * k * np.arange(period)[None, :] / period
    forward = np.concatenate([np.cos(angle) * used, np.sin(angle) * used], axis=0)
    weight = np.where((k == 0) | (k == period // 2), 1.0, 2.0) / period
    inverse = np.concatenate([forward[:bins] * weight, -forward[bins:] * weight], axis=0)
    return forward.astype(np.float32), inverse[:, :shifts].T.astype(np.float32)


def score_kernel(taps, shifts, places, more, last, *refs):
    n = len(places)
    mine, theirs, forward, inverse = refs[:4]
    packed = refs[4 : 4 + n]
    at = 4 + n + more
    prev_ref, outs = refs[4 + n : at], refs[at : at + 1 + last]
    gains, ints_v, ints, tails, rows_f, rows_b, sums, scales, sem = refs[at + 1 + last :]
    samples, channels = mine.shape
    width = packed[0].shape[1]
    groups = width // LANES
    whole_tiles = channels // LANES
    rest = channels - whole_tiles * LANES
    chan = lax.axis_index("chan")
    blocks = shifts // 8
    steps = taps // 8
    lane_row = lax.broadcasted_iota(jnp.int32, (1, LANES), 1)

    for i in range(n):
        meta = packed[i][taps:, :LANES].astype(jnp.float32)
        ints_v[i : i + 1, :] = (meta[:1] * 256.0 + meta[1:2]).astype(jnp.int32)
    to_scalars = pltpu.make_async_copy(ints_v, ints, sem)
    to_scalars.start()
    for i in range(n):
        for g in range(groups):
            block = packed[i][:taps, g * LANES : (g + 1) * LANES].astype(jnp.float32)
            tiles = [block[8 * a : 8 * a + 8] for a in range(steps)]
            energy = jnp.zeros((8, LANES), jnp.float32)
            for a in range(0, steps, 2):
                energy = energy + (tiles[a] * tiles[a] + tiles[a + 1] * tiles[a + 1])
            gains[i * groups + g : i * groups + g + 1, :] = jnp.sum(energy, axis=0, keepdims=True)
    if rest:
        tails[0, :, :rest] = mine[:, whole_tiles * LANES :]
        tails[1, :, :rest] = theirs[:, whole_tiles * LANES :]
    rows_f[(samples // 8) * 8 :, :] = jnp.zeros_like(rows_f[(samples // 8) * 8 :, :])
    to_scalars.wait()
    for i in range(n):
        count = jnp.full((1, LANES), ints[i, 1], jnp.int32)
        ratio = jnp.sqrt(taps / count.astype(jnp.float32)) * (1.0 / taps)
        for g in range(groups):
            at = i * groups + g
            gain = lax.rsqrt(gains[at : at + 1, :] / taps + 1e-06) * ratio
            gains[at : at + 1, :] = jnp.where(lane_row + (chan * width + g * LANES) < count, gain, 0.0)

    wide = lax.broadcasted_iota(jnp.int32, (samples, LANES), 1)

    def turned(low, high, turn):
        mixed = jnp.where(wide < turn, high.astype(jnp.float32), low.astype(jnp.float32))
        return pltpu.roll(mixed, (LANES - turn) & (LANES - 1), 1)

    def item(index, _):
        i, g = index // groups, index % groups
        first = ints[i, 0] + chan * width + g * LANES
        split = channels - first
        half = jnp.where(split > 0, 0, 1)
        local = first - half * channels
        tile = local >> 7
        fast = ((split >= LANES) | (split <= 0)) & (tile + 1 < whole_tiles)

        for source, here in ((mine, half == chan), (theirs, half != chan)):

            @pl.when(fast & here)
            def _():
                at = pl.multiple_of(tile * LANES, LANES)
                rows_f[:samples, :] = turned(
                    source[:, pl.ds(at, LANES)], source[:, pl.ds(at + LANES, LANES)], local & (LANES - 1)
                )

        @pl.when(jnp.logical_not(fast))
        def _():
            sides = []
            for side in range(2):
                begin = first - side * channels
                turn = begin & (LANES - 1)
                found = []
                for m in range(2):
                    want = (begin >> 7) + m
                    at = pl.multiple_of(jnp.clip(want, 0, whole_tiles - 1) * LANES, LANES)
                    value = jnp.where(
                        chan == side,
                        mine[:, pl.ds(at, LANES)].astype(jnp.float32),
                        theirs[:, pl.ds(at, LANES)].astype(jnp.float32),
                    )
                    if rest:
                        tail = tails[jnp.where(chan == side, 0, 1)].astype(jnp.float32)
                        value = jnp.where(want >= whole_tiles, tail, value)
                    found.append(value)
                sides.append(turned(found[0], found[1], turn))
            rows_f[:samples, :] = jnp.where(wide < split, sides[0], sides[1])

        rows_b[i, :, pl.ds(pl.multiple_of(g * LANES, LANES), LANES)] = rows_f[...].astype(jnp.bfloat16)

        origin = index >> 16
        level = [rows_f[8 * m : 8 * m + 8, :] for m in range(steps + blocks)]
        level = [v * v for v in level]
        span = 1
        while span < steps:
            level = [level[m] + level[m + span] for m in range(len(level) - span)]
            span *= 2
        for m in range(blocks + 1):
            sums[pl.ds(origin + PITCH * m, 8), :] = level[m]
        near = [sums[pl.ds(m + m // 8, 8, stride=PITCH), :] for m in range(15)]
        before, after = [near[7]], [near[8]]
        for m in range(1, 8):
            before.append(before[-1] + near[7 - m])
        for m in range(1, 7):
            after.append(after[-1] + near[8 + m])
        window = [before[7]] + [before[7 - b] + after[b - 1] for b in range(1, 8)]
        gain = gains[pl.ds(index, 8, stride=0), :]
        for b in range(8):
            scale = lax.rsqrt(window[b] / taps + 1e-06) * gain
            scales[pl.ds(index * shifts + b, 8, stride=8), :] = scale
        return 0

    lax.fori_loop(0, n * groups, item, 0)
    def dot(left, right):
        return jnp.dot(left, right, preferred_element_type=jnp.float32)

    bins = forward.shape[0] // 2
    forward_terms = three_terms(forward[...])
    inverse_terms = jnp.concatenate(three_terms(inverse[...]), axis=0)
    totals = []
    for i in range(n):
        spectra = []
        for value, depth in ((rows_b[i], rows_b.shape[1]), (packed[i][:taps, :], taps)):
            terms = [dot(term[:, :depth], value) for term in forward_terms]
            spectra.append(terms[2] + terms[1] + terms[0])
        rec, tmpl = spectra
        rec_c, rec_s, tmpl_c, tmpl_s = rec[:bins], rec[bins:], tmpl[:bins], tmpl[bins:]
        spectrum = jnp.concatenate(
            [rec_c * tmpl_c + rec_s * tmpl_s, rec_c * tmpl_s - rec_s * tmpl_c], axis=0
        )
        products = [
            dot(inverse_terms[: (3 - m) * shifts, :], term)
            for m, term in enumerate(three_terms(spectrum))
        ]
        small = products[0][2 * shifts :] + products[1][shifts:] + products[2]
        lag = small + (products[0][shifts : 2 * shifts] + products[1][:shifts]) + products[0][:shifts]
        totals.append(
            sum(
                lag[:, g * LANES : (g + 1) * LANES]
                * scales[(i * groups + g) * shifts : (i * groups + g + 1) * shifts, :]
                for g in range(groups)
            )
        )

    ones = jnp.ones((8, LANES), jnp.bfloat16)
    stacked = sum(
        lax.dot_general(ones, term, (((1,), (1,)), ((), ())), preferred_element_type=jnp.float32)
        for term in three_terms(jnp.concatenate(totals, axis=0))
    )
    result = prev_ref[0][...] if more else jnp.zeros(outs[0].shape[:1] + (shifts,), jnp.float32)
    sub = lax.broadcasted_iota(jnp.int32, result.shape, 0)
    blk = lax.axis_index("blk")
    for i in range(n):
        row = places[i][0] if places[i][1] else blk ^ places[i][0]
        result = jnp.where(sub == row, stacked[:1, i * shifts : (i + 1) * shifts], result)
    if not last:
        outs[0][...] = result
        return
    left, right = result[:, : shifts // 2], result[:, shifts // 2 :]
    outs[0][...] = jnp.where(chan == 0, left, right)
    outs[1][...] = jnp.where(chan == 0, right, left)


def score(records, tables, packed, places, templates, taps, shifts, prev=(), last=True):
    n = len(packed)
    samples, channels = records[0].shape
    width = packed[0].shape[1]
    groups = width // LANES
    items = n * groups
    padded = tables[0].shape[1]
    vmem = pl.BlockSpec(memory_space=pltpu.VMEM)
    if last:
        out_shape = (jax.ShapeDtypeStruct((templates, shifts // 2), jnp.float32),) * 2
    else:
        out_shape = (jax.ShapeDtypeStruct((templates, shifts), jnp.float32),)
    return pl.pallas_call(
        functools.partial(score_kernel, taps, shifts, places, len(prev), int(last)),
        out_shape=out_shape,
        in_specs=[vmem] * (4 + n + len(prev)),
        out_specs=(vmem,) * len(out_shape),
        scratch_shapes=[
            pltpu.VMEM((-(-items // 8) * 8 + 8, LANES), jnp.float32),
            pltpu.VMEM((n, LANES), jnp.int32),
            pltpu.SMEM((n, LANES), jnp.int32),
            pltpu.VMEM((2, samples, LANES), records[0].dtype),
            pltpu.VMEM((padded, LANES), jnp.float32),
            pltpu.VMEM((n, padded, width), jnp.bfloat16),
            pltpu.VMEM(((shifts // 8 + 2) * PITCH, LANES), jnp.float32),
            pltpu.VMEM((items * shifts + 8, LANES), jnp.float32),
            pltpu.SemaphoreType.DMA,
        ],
        compiler_params=pltpu.CompilerParams(vmem_limit_bytes=32 * 2**20),
        cost_estimate=pl.CostEstimate(
            flops=2 * n * width * taps * shifts, bytes_accessed=n * width * samples * 4, transcendentals=0
        ),
        name="score",
    )(*records, *tables, *packed, *prev)


def exchange(value, axis, size, mask):
    return lax.ppermute(value, axis, [(i, i ^ mask) for i in range(size)])


def on_device(mesh_shape, record, templates, offsets, counts):
    blk = mesh_shape["blk"]
    taps = templates.shape[2]
    shifts = record.shape[2] - taps + 1
    packed, own = pack(templates[0], offsets, counts)
    mine = jnp.transpose(record[0])
    period = -(-record.shape[2] // 64) * 64
    tables = tuple(jnp.asarray(table) for table in fourier_tables(period, shifts))
    if blk == CHUNK:
        held = {0: own}
        for mask in (4, 1, 2):
            held[mask] = exchange(packed, "blk", blk, mask)
        theirs = exchange(mine, "chan", 2, 1)

        def step(masks, rows, last=False):
            return score(
                (mine, theirs), tables, [held[m] for m in masks], [(m, False) for m in masks],
                blk, taps, shifts, rows, last,
            )

        rows = step((0,), ())
        rows, *near = lax.optimization_barrier((rows, held[4], held[1], held[2]))
        held[4], held[1], held[2] = near
        held[6] = exchange(held[4], "blk", blk, 2)
        held[5] = exchange(held[4], "blk", blk, 1)
        held[3] = exchange(held[1], "blk", blk, 2)
        rows = step((1, 2, 4), rows)
        rows, held[6] = lax.optimization_barrier((rows, held[6]))
        held[7] = exchange(held[6], "blk", blk, 1)
        rows = step((3, 5, 6), rows)
        rows = step((7,), rows, True)
        keep, send = rows
    else:
        theirs = exchange(mine, "chan", 2, 1)
        every = lax.all_gather(packed, "blk", axis=0, tiled=False)
        keeps, sends = [], []
        for at in range(0, blk, CHUNK):
            size = min(CHUNK, blk - at)
            keep, send = score(
                (mine, theirs), tables, [every[at + i] for i in range(size)],
                [(i, True) for i in range(size)], size, taps, shifts,
            )
            keeps.append(keep)
            sends.append(send)
        keep, send = jnp.concatenate(keeps, axis=0), jnp.concatenate(sends, axis=0)
    return (keep + exchange(send, "chan", 2, 1))[None]


def solution(mesh):
    in_specs = (P(("grp", "blk"), "chan", None), P("blk", "chan", None), P("blk"), P("blk"))
    out_specs = P(("grp", "blk"), None, "chan")
    return jax.shard_map(
        functools.partial(on_device, dict(mesh.shape)),
        mesh=mesh, in_specs=in_specs, out_specs=out_specs, check_vma=False,
    )
```

```python
import functools

import jax
import jax.numpy as jnp
import numpy as np
from jax import lax
from jax.experimental import pallas as pl
from jax.experimental.pallas import tpu as pltpu
from jax.sharding import PartitionSpec as P

LANES = 128
META = 8
CHUNK = 8
PITCH = 9


def pack_kernel(off_ref, cnt_ref, tmpl_ref, out_ref, own_ref):
    rows, taps = tmpl_ref.shape
    lane = lax.broadcasted_iota(jnp.int32, (META, rows), 1)
    level = lax.broadcasted_iota(jnp.int32, (META, rows), 0)
    value = jnp.where(lane == 0, off_ref[0], cnt_ref[0])
    meta = jnp.where(level == 0, value >> 8, value & 255).astype(jnp.float32).astype(out_ref.dtype)
    turned = jnp.transpose(tmpl_ref[...].astype(jnp.float32)).astype(out_ref.dtype)
    for ref in (out_ref, own_ref):
        ref[:taps, :] = turned
        ref[taps:, :] = meta


def pack(templates, offsets, counts):
    rows, taps = templates.shape
    smem = pl.BlockSpec(memory_space=pltpu.SMEM)
    vmem = pl.BlockSpec(memory_space=pltpu.VMEM)
    return pl.pallas_call(
        pack_kernel,
        out_shape=(jax.ShapeDtypeStruct((taps + META, rows), templates.dtype),) * 2,
        in_specs=[smem, smem, vmem],
        out_specs=(vmem, vmem),
        cost_estimate=pl.CostEstimate(flops=4 * 10**9, bytes_accessed=10**7, transcendentals=0),
        compiler_params=pltpu.CompilerParams(vmem_limit_bytes=4 * 2**20),
        name="pack",
    )(offsets, counts, templates)


def three_terms(value):
    terms = []
    for _ in range(3):
        terms.append(value.astype(jnp.bfloat16))
        value = value - terms[-1].astype(jnp.float32)
    return terms


def fourier_tables(period, shifts):
    bins = -(-(period // 2 + 1) // 8) * 8
    k = np.arange(bins)[:, None]
    used = k <= period // 2
    angle = 2 * np.pi * k * np.arange(period)[None, :] / period
    forward = np.concatenate([np.cos(angle) * used, np.sin(angle) * used], axis=0)
    weight = np.where((k == 0) | (k == period // 2), 1.0, 2.0) / period
    inverse = np.concatenate([forward[:bins] * weight, -forward[bins:] * weight], axis=0)
    return forward.astype(np.float32), inverse[:, :shifts].T.astype(np.float32)


def score_kernel(taps, shifts, places, more, last, split, *refs):
    n = len(places)
    mine, theirs, forward, inverse = refs[:4]
    packed = refs[4 : 4 + n]
    at = 4 + n + more
    prev_ref, outs = refs[4 + n : at], refs[at : at + 1 + last + 2 * split]
    gains, ints, tails, rows_f, rows_b, sums, scales = refs[at + len(outs) :]
    samples, channels = mine.shape
    width = packed[0].shape[1]
    groups = width // LANES
    whole_tiles = channels // LANES
    rest = channels - whole_tiles * LANES
    chan = lax.axis_index("chan")
    blocks = shifts // 8
    steps = taps // 8
    lane_row = lax.broadcasted_iota(jnp.int32, (1, LANES), 1)

    for i in range(n):
        meta = packed[i][taps:, :LANES].astype(jnp.float32)
        numbers = (meta[:1] * 256.0 + meta[1:2]).astype(jnp.int32)
        ints[i, 0] = numbers[0, 0]
        ints[i, 1] = numbers[0, 1]
    for i in range(n):
        for g in range(groups):
            block = packed[i][:taps, g * LANES : (g + 1) * LANES].astype(jnp.float32)
            tiles = [block[8 * a : 8 * a + 8] for a in range(steps)]
            energy = jnp.zeros((8, LANES), jnp.float32)
            for a in range(0, steps, 2):
                energy = energy + (tiles[a] * tiles[a] + tiles[a + 1] * tiles[a + 1])
            gains[i * groups + g : i * groups + g + 1, :] = jnp.sum(energy, axis=0, keepdims=True)
    if rest:
        tails[0, :, :rest] = mine[:, whole_tiles * LANES :]
        tails[1, :, :rest] = theirs[:, whole_tiles * LANES :]
    rows_f[(samples // 8) * 8 :, :] = jnp.zeros_like(rows_f[(samples // 8) * 8 :, :])
    for i in range(n):
        count = jnp.full((1, LANES), ints[i, 1], jnp.int32)
        ratio = jnp.sqrt(taps / count.astype(jnp.float32)) * (1.0 / taps)
        for g in range(groups):
            at = i * groups + g
            gain = lax.rsqrt(gains[at : at + 1, :] / taps + 1e-06) * ratio
            gains[at : at + 1, :] = jnp.where(lane_row + (chan * width + g * LANES) < count, gain, 0.0)

    wide = lax.broadcasted_iota(jnp.int32, (samples, LANES), 1)

    def turned(low, high, turn):
        mixed = jnp.where(wide < turn, high.astype(jnp.float32), low.astype(jnp.float32))
        return pltpu.roll(mixed, (LANES - turn) & (LANES - 1), 1)

    def item(index, _):
        i, g = index // groups, index % groups
        first = ints[i, 0] + chan * width + g * LANES
        split = channels - first
        half = jnp.where(split > 0, 0, 1)
        local = first - half * channels
        tile = local >> 7
        fast = ((split >= LANES) | (split <= 0)) & (tile + 1 < whole_tiles)

        for source, here in ((mine, half == chan), (theirs, half != chan)):

            @pl.when(fast & here)
            def _():
                at = pl.multiple_of(tile * LANES, LANES)
                rows_f[:samples, :] = turned(
                    source[:, pl.ds(at, LANES)], source[:, pl.ds(at + LANES, LANES)], local & (LANES - 1)
                )

        @pl.when(jnp.logical_not(fast))
        def _():
            sides = []
            for side in range(2):
                begin = first - side * channels
                turn = begin & (LANES - 1)
                found = []
                for m in range(2):
                    want = (begin >> 7) + m
                    at = pl.multiple_of(jnp.clip(want, 0, whole_tiles - 1) * LANES, LANES)
                    value = jnp.where(
                        chan == side,
                        mine[:, pl.ds(at, LANES)].astype(jnp.float32),
                        theirs[:, pl.ds(at, LANES)].astype(jnp.float32),
                    )
                    if rest:
                        tail = tails[jnp.where(chan == side, 0, 1)].astype(jnp.float32)
                        value = jnp.where(want >= whole_tiles, tail, value)
                    found.append(value)
                sides.append(turned(found[0], found[1], turn))
            rows_f[:samples, :] = jnp.where(wide < split, sides[0], sides[1])

        rows_b[i, :, pl.ds(pl.multiple_of(g * LANES, LANES), LANES)] = rows_f[...].astype(jnp.bfloat16)

        origin = index >> 16
        level = [rows_f[8 * m : 8 * m + 8, :] for m in range(steps + blocks)]
        level = [v * v for v in level]
        span = 1
        while span < steps:
            level = [level[m] + level[m + span] for m in range(len(level) - span)]
            span *= 2
        for m in range(blocks + 1):
            sums[pl.ds(origin + PITCH * m, 8), :] = level[m]
        near = [sums[pl.ds(m + m // 8, 8, stride=PITCH), :] for m in range(15)]
        before, after = [near[7]], [near[8]]
        for m in range(1, 8):
            before.append(before[-1] + near[7 - m])
        for m in range(1, 7):
            after.append(after[-1] + near[8 + m])
        window = [before[7]] + [before[7 - b] + after[b - 1] for b in range(1, 8)]
        gain = gains[pl.ds(index, 8, stride=0), :]
        for b in range(8):
            scale = lax.rsqrt(window[b] / taps + 1e-06) * gain
            scales[pl.ds(index * shifts + b, 8, stride=8), :] = scale
        return 0

    lax.fori_loop(0, n * groups, item, 0)
    def dot(left, right):
        return jnp.dot(left, right, preferred_element_type=jnp.float32)

    if split:
        for table, ref in zip((forward, inverse), outs[-2:]):
            ref[...] = jnp.concatenate(three_terms(table[...]), axis=0)
        forward, inverse = outs[-2:]
    tall = forward.shape[0] // 3
    bins = tall // 2
    totals = []
    for i in range(n):
        spectra = []
        for value, depth in ((rows_b[i], rows_b.shape[1]), (packed[i][:taps, :], taps)):
            terms = [dot(forward[m * tall : (m + 1) * tall, :depth], value) for m in range(3)]
            spectra.append(terms[2] + terms[1] + terms[0])
        rec, tmpl = spectra
        rec_c, rec_s, tmpl_c, tmpl_s = rec[:bins], rec[bins:], tmpl[:bins], tmpl[bins:]
        spectrum = jnp.concatenate(
            [rec_c * tmpl_c + rec_s * tmpl_s, rec_c * tmpl_s - rec_s * tmpl_c], axis=0
        )
        products = [
            dot(inverse[: (3 - m) * shifts, :], term)
            for m, term in enumerate(three_terms(spectrum))
        ]
        small = products[0][2 * shifts :] + products[1][shifts:] + products[2]
        lag = small + (products[0][shifts : 2 * shifts] + products[1][:shifts]) + products[0][:shifts]
        totals.append(
            sum(
                lag[:, g * LANES : (g + 1) * LANES]
                * scales[(i * groups + g) * shifts : (i * groups + g + 1) * shifts, :]
                for g in range(groups)
            )
        )

    ones = jnp.ones((8, LANES), jnp.bfloat16)
    stacked = sum(
        lax.dot_general(ones, term, (((1,), (1,)), ((), ())), preferred_element_type=jnp.float32)
        for term in three_terms(jnp.concatenate(totals, axis=0))
    )
    result = prev_ref[0][...] if more else jnp.zeros(outs[0].shape[:1] + (shifts,), jnp.float32)
    sub = lax.broadcasted_iota(jnp.int32, result.shape, 0)
    blk = lax.axis_index("blk")
    for i in range(n):
        row = places[i][0] if places[i][1] else blk ^ places[i][0]
        result = jnp.where(sub == row, stacked[:1, i * shifts : (i + 1) * shifts], result)
    if not last:
        outs[0][...] = result
        return
    left, right = result[:, : shifts // 2], result[:, shifts // 2 :]
    outs[0][...] = jnp.where(chan == 0, left, right)
    outs[1][...] = jnp.where(chan == 0, right, left)


def score(records, tables, packed, places, templates, taps, shifts, prev=(), last=True, split=True):
    n = len(packed)
    samples, channels = records[0].shape
    width = packed[0].shape[1]
    groups = width // LANES
    items = n * groups
    padded = tables[0].shape[1]
    vmem = pl.BlockSpec(memory_space=pltpu.VMEM)
    if last:
        out_shape = (jax.ShapeDtypeStruct((templates, shifts // 2), jnp.float32),) * 2
    else:
        out_shape = (jax.ShapeDtypeStruct((templates, shifts), jnp.float32),)
    if split:
        out_shape += tuple(
            jax.ShapeDtypeStruct((3 * table.shape[0], table.shape[1]), jnp.bfloat16) for table in tables
        )
    return pl.pallas_call(
        functools.partial(score_kernel, taps, shifts, places, len(prev), int(last), int(split)),
        out_shape=out_shape,
        in_specs=[vmem] * (4 + n + len(prev)),
        out_specs=(vmem,) * len(out_shape),
        scratch_shapes=[
            pltpu.VMEM((-(-items // 8) * 8 + 8, LANES), jnp.float32),
            pltpu.SMEM((n, 2), jnp.int32),
            pltpu.VMEM((2, samples, LANES), records[0].dtype),
            pltpu.VMEM((padded, LANES), jnp.float32),
            pltpu.VMEM((n, padded, width), jnp.bfloat16),
            pltpu.VMEM(((shifts // 8 + 2) * PITCH, LANES), jnp.float32),
            pltpu.VMEM((items * shifts + 8, LANES), jnp.float32),
        ],
        compiler_params=pltpu.CompilerParams(vmem_limit_bytes=32 * 2**20),
        cost_estimate=pl.CostEstimate(
            flops=2 * n * width * taps * shifts, bytes_accessed=n * width * samples * 4, transcendentals=0
        ),
        name="score",
    )(*records, *tables, *packed, *prev)


def exchange(value, axis, size, mask):
    return lax.ppermute(value, axis, [(i, i ^ mask) for i in range(size)])


def on_device(mesh_shape, record, templates, offsets, counts):
    blk = mesh_shape["blk"]
    taps = templates.shape[2]
    shifts = record.shape[2] - taps + 1
    packed, own = pack(templates[0], offsets, counts)
    mine = jnp.transpose(record[0])
    period = -(-record.shape[2] // 64) * 64
    tables = tuple(jnp.asarray(table) for table in fourier_tables(period, shifts))
    if blk == CHUNK:
        held = {0: own}
        for mask in (4, 1, 2):
            held[mask] = exchange(packed, "blk", blk, mask)
        theirs = exchange(mine, "chan", 2, 1)

        def step(masks, rows, last=False, split=False):
            return score(
                (mine, theirs), tables, [held[m] for m in masks], [(m, False) for m in masks],
                blk, taps, shifts, rows, last, split,
            )

        rows, *tables = step((0,), (), split=True)
        near = lax.optimization_barrier((rows, *(held[m] for m in (2, 1, 4))))
        rows = near[:1]
        held.update(zip((2, 1, 4), near[1:]))
        held[6] = exchange(held[4], "blk", blk, 2)
        held[5] = exchange(held[4], "blk", blk, 1)
        held[3] = exchange(held[1], "blk", blk, 2)
        rows = step((1, 2, 4), rows)
        rows, held[6] = lax.optimization_barrier((rows, held[6]))
        held[7] = exchange(held[6], "blk", blk, 1)
        rows = step((3, 5, 6), rows)
        rows = step((7,), rows, True)
        keep, send = rows
    else:
        theirs = exchange(mine, "chan", 2, 1)
        every = lax.all_gather(packed, "blk", axis=0, tiled=False)
        keeps, sends = [], []
        for at in range(0, blk, CHUNK):
            size = min(CHUNK, blk - at)
            keep, send, *_ = score(
                (mine, theirs), tables, [every[at + i] for i in range(size)],
                [(i, True) for i in range(size)], size, taps, shifts,
            )
            keeps.append(keep)
            sends.append(send)
        keep, send = jnp.concatenate(keeps, axis=0), jnp.concatenate(sends, axis=0)
    return (keep + exchange(send, "chan", 2, 1))[None]


def solution(mesh):
    in_specs = (P(("grp", "blk"), "chan", None), P("blk", "chan", None), P("blk"), P("blk"))
    out_specs = P(("grp", "blk"), None, "chan")
    return jax.shard_map(
        functools.partial(on_device, dict(mesh.shape)),
        mesh=mesh, in_specs=in_specs, out_specs=out_specs, check_vma=False,
    )
```

```python
import functools

import jax
import jax.numpy as jnp
import numpy as np
from jax import lax
from jax.experimental import pallas as pl
from jax.experimental.pallas import tpu as pltpu
from jax.sharding import PartitionSpec as P

LANES = 128
META = 8
CHUNK = 8
PITCH = 9


def pack_kernel(off_ref, cnt_ref, tmpl_ref, out_ref, own_ref):
    rows, taps = tmpl_ref.shape
    lane = lax.broadcasted_iota(jnp.int32, (META, rows), 1)
    level = lax.broadcasted_iota(jnp.int32, (META, rows), 0)
    value = jnp.where(lane == 0, off_ref[0], cnt_ref[0])
    meta = jnp.where(level == 0, value >> 8, value & 255).astype(jnp.float32).astype(out_ref.dtype)
    turned = jnp.transpose(tmpl_ref[...].astype(jnp.float32)).astype(out_ref.dtype)
    for ref in (out_ref, own_ref):
        ref[:taps, :] = turned
        ref[taps:, :] = meta


def pack(templates, offsets, counts):
    rows, taps = templates.shape
    smem = pl.BlockSpec(memory_space=pltpu.SMEM)
    vmem = pl.BlockSpec(memory_space=pltpu.VMEM)
    return pl.pallas_call(
        pack_kernel,
        out_shape=(jax.ShapeDtypeStruct((taps + META, rows), templates.dtype),) * 2,
        in_specs=[smem, smem, vmem],
        out_specs=(vmem, vmem),
        cost_estimate=pl.CostEstimate(flops=4 * 10**9, bytes_accessed=10**7, transcendentals=0),
        compiler_params=pltpu.CompilerParams(vmem_limit_bytes=4 * 2**20),
        name="pack",
    )(offsets, counts, templates)


def three_terms(value):
    terms = []
    for _ in range(3):
        terms.append(value.astype(jnp.bfloat16))
        value = value - terms[-1].astype(jnp.float32)
    return terms


def fourier_tables(period, shifts):
    bins = -(-(period // 2 + 1) // 8) * 8
    k = np.arange(bins)[:, None]
    used = k <= period // 2
    angle = 2 * np.pi * k * np.arange(period)[None, :] / period
    forward = np.concatenate([np.cos(angle) * used, np.sin(angle) * used], axis=0)
    weight = np.where((k == 0) | (k == period // 2), 1.0, 2.0) / period
    inverse = np.concatenate([forward[:bins] * weight, -forward[bins:] * weight], axis=0)
    return forward.astype(np.float32), inverse[:, :shifts].T.astype(np.float32)


def score_kernel(taps, shifts, places, more, last, split, *refs):
    n = len(places)
    mine, theirs, forward, inverse = refs[:4]
    packed = refs[4 : 4 + n]
    at = 4 + n + more
    prev_ref, outs = refs[4 + n : at], refs[at : at + 1 + last + 2 * split]
    gains, ints, tails, rows_f, rows_b, sums, scales = refs[at + len(outs) :]
    samples, channels = mine.shape
    width = packed[0].shape[1]
    groups = width // LANES
    whole_tiles = channels // LANES
    rest = channels - whole_tiles * LANES
    chan = lax.axis_index("chan")
    blocks = shifts // 8
    steps = taps // 8
    lane_row = lax.broadcasted_iota(jnp.int32, (1, LANES), 1)

    for i in range(n):
        meta = packed[i][taps:, :LANES].astype(jnp.float32)
        numbers = (meta[:1] * 256.0 + meta[1:2]).astype(jnp.int32)
        ints[i, 0] = numbers[0, 0]
        ints[i, 1] = numbers[0, 1]
    for i in range(n):
        for g in range(groups):
            block = packed[i][:taps, g * LANES : (g + 1) * LANES].astype(jnp.float32)
            tiles = [block[8 * a : 8 * a + 8] for a in range(steps)]
            energy = jnp.zeros((8, LANES), jnp.float32)
            for a in range(0, steps, 2):
                energy = energy + (tiles[a] * tiles[a] + tiles[a + 1] * tiles[a + 1])
            gains[i * groups + g : i * groups + g + 1, :] = jnp.sum(energy, axis=0, keepdims=True)
    if rest:
        tails[0, :, :rest] = mine[:, whole_tiles * LANES :]
        tails[1, :, :rest] = theirs[:, whole_tiles * LANES :]
    rows_f[(samples // 8) * 8 :, :] = jnp.zeros_like(rows_f[(samples // 8) * 8 :, :])
    for i in range(n):
        count = jnp.full((1, LANES), ints[i, 1], jnp.int32)
        ratio = lax.rsqrt(count.astype(jnp.float32)) * (taps**0.5 / taps)
        for g in range(groups):
            at = i * groups + g
            gain = lax.rsqrt(gains[at : at + 1, :] * (1.0 / taps) + 1e-06) * ratio
            gains[at : at + 1, :] = jnp.where(lane_row + (chan * width + g * LANES) < count, gain, 0.0)

    wide = lax.broadcasted_iota(jnp.int32, (samples, LANES), 1)

    def turned(low, high, turn):
        mixed = jnp.where(wide < turn, high.astype(jnp.float32), low.astype(jnp.float32))
        return pltpu.roll(mixed, (LANES - turn) & (LANES - 1), 1)

    def item(index, _):
        i, g = index // groups, index % groups
        first = ints[i, 0] + chan * width + g * LANES
        split = channels - first
        half = jnp.where(split > 0, 0, 1)
        local = first - half * channels
        tile = local >> 7
        fast = ((split >= LANES) | (split <= 0)) & (tile + 1 < whole_tiles)

        for source, here in ((mine, half == chan), (theirs, half != chan)):

            @pl.when(fast & here)
            def _():
                at = pl.multiple_of(tile * LANES, LANES)
                rows_f[:samples, :] = turned(
                    source[:, pl.ds(at, LANES)], source[:, pl.ds(at + LANES, LANES)], local & (LANES - 1)
                )

        @pl.when(jnp.logical_not(fast))
        def _():
            sides = []
            for side in range(2):
                begin = first - side * channels
                turn = begin & (LANES - 1)
                found = []
                for m in range(2):
                    want = (begin >> 7) + m
                    at = pl.multiple_of(jnp.clip(want, 0, whole_tiles - 1) * LANES, LANES)
                    value = jnp.where(
                        chan == side,
                        mine[:, pl.ds(at, LANES)].astype(jnp.float32),
                        theirs[:, pl.ds(at, LANES)].astype(jnp.float32),
                    )
                    if rest:
                        tail = tails[jnp.where(chan == side, 0, 1)].astype(jnp.float32)
                        value = jnp.where(want >= whole_tiles, tail, value)
                    found.append(value)
                sides.append(turned(found[0], found[1], turn))
            rows_f[:samples, :] = jnp.where(wide < split, sides[0], sides[1])

        rows_b[i, :, pl.ds(pl.multiple_of(g * LANES, LANES), LANES)] = rows_f[...].astype(jnp.bfloat16)

        origin = index >> 16
        level = [rows_f[8 * m : 8 * m + 8, :] for m in range(steps + blocks)]
        level = [v * v for v in level]
        span = 1
        while span < steps:
            level = [level[m] + level[m + span] for m in range(len(level) - span)]
            span *= 2
        for m in range(blocks + 1):
            sums[pl.ds(origin + PITCH * m, 8), :] = level[m]
        near = [sums[pl.ds(m + m // 8, 8, stride=PITCH), :] for m in range(15)]
        before, after = [near[7]], [near[8]]
        for m in range(1, 8):
            before.append(before[-1] + near[7 - m])
        for m in range(1, 7):
            after.append(after[-1] + near[8 + m])
        window = [before[7]] + [before[7 - b] + after[b - 1] for b in range(1, 8)]
        gain = gains[pl.ds(index, 8, stride=0), :]
        for b in range(8):
            scale = lax.rsqrt(window[b] * (1.0 / taps) + 1e-06) * gain
            scales[pl.ds(index * shifts + b, 8, stride=8), :] = scale
        return 0

    lax.fori_loop(0, n * groups, item, 0)
    def dot(left, right):
        return jnp.dot(left, right, preferred_element_type=jnp.float32)

    if split:
        for table, ref in zip((forward, inverse), outs[-2:]):
            ref[...] = jnp.concatenate(three_terms(table[...]), axis=0)
        forward, inverse = outs[-2:]
    tall = forward.shape[0] // 3
    bins = tall // 2
    totals = []
    for i in range(n):
        spectra = []
        for value, depth in ((rows_b[i], rows_b.shape[1]), (packed[i][:taps, :], taps)):
            terms = dot(forward[:, :depth], value)
            spectra.append(terms[2 * tall :] + terms[tall : 2 * tall] + terms[:tall])
        rec, tmpl = spectra
        rec_c, rec_s, tmpl_c, tmpl_s = rec[:bins], rec[bins:], tmpl[:bins], tmpl[bins:]
        spectrum = jnp.concatenate(
            [rec_c * tmpl_c + rec_s * tmpl_s, rec_c * tmpl_s - rec_s * tmpl_c], axis=0
        )
        products = [
            dot(inverse[: (3 - m) * shifts, :], term)
            for m, term in enumerate(three_terms(spectrum))
        ]
        small = products[0][2 * shifts :] + products[1][shifts:] + products[2]
        lag = small + (products[0][shifts : 2 * shifts] + products[1][:shifts]) + products[0][:shifts]
        totals.append(
            sum(
                lag[:, g * LANES : (g + 1) * LANES]
                * scales[(i * groups + g) * shifts : (i * groups + g + 1) * shifts, :]
                for g in range(groups)
            )
        )

    ones = jnp.ones((8, LANES), jnp.bfloat16)
    stacked = sum(
        lax.dot_general(ones, term, (((1,), (1,)), ((), ())), preferred_element_type=jnp.float32)
        for term in three_terms(jnp.concatenate(totals, axis=0))
    )
    result = prev_ref[0][...] if more else jnp.zeros(outs[0].shape[:1] + (shifts,), jnp.float32)
    sub = lax.broadcasted_iota(jnp.int32, result.shape, 0)
    blk = lax.axis_index("blk")
    for i in range(n):
        row = places[i][0] if places[i][1] else blk ^ places[i][0]
        result = jnp.where(sub == row, stacked[:1, i * shifts : (i + 1) * shifts], result)
    if not last:
        outs[0][...] = result
        return
    left, right = result[:, : shifts // 2], result[:, shifts // 2 :]
    outs[0][...] = jnp.where(chan == 0, left, right)
    outs[1][...] = jnp.where(chan == 0, right, left)


def score(records, tables, packed, places, templates, taps, shifts, prev=(), last=True, split=True):
    n = len(packed)
    samples, channels = records[0].shape
    width = packed[0].shape[1]
    groups = width // LANES
    items = n * groups
    padded = tables[0].shape[1]
    vmem = pl.BlockSpec(memory_space=pltpu.VMEM)
    if last:
        out_shape = (jax.ShapeDtypeStruct((templates, shifts // 2), jnp.float32),) * 2
    else:
        out_shape = (jax.ShapeDtypeStruct((templates, shifts), jnp.float32),)
    if split:
        out_shape += tuple(
            jax.ShapeDtypeStruct((3 * table.shape[0], table.shape[1]), jnp.bfloat16) for table in tables
        )
    return pl.pallas_call(
        functools.partial(score_kernel, taps, shifts, places, len(prev), int(last), int(split)),
        out_shape=out_shape,
        in_specs=[vmem] * (4 + n + len(prev)),
        out_specs=(vmem,) * len(out_shape),
        scratch_shapes=[
            pltpu.VMEM((-(-items // 8) * 8 + 8, LANES), jnp.float32),
            pltpu.SMEM((n, 2), jnp.int32),
            pltpu.VMEM((2, samples, LANES), records[0].dtype),
            pltpu.VMEM((padded, LANES), jnp.float32),
            pltpu.VMEM((n, padded, width), jnp.bfloat16),
            pltpu.VMEM(((shifts // 8 + 2) * PITCH, LANES), jnp.float32),
            pltpu.VMEM((items * shifts + 8, LANES), jnp.float32),
        ],
        compiler_params=pltpu.CompilerParams(vmem_limit_bytes=32 * 2**20),
        cost_estimate=pl.CostEstimate(
            flops=2 * n * width * taps * shifts, bytes_accessed=n * width * samples * 4, transcendentals=0
        ),
        name="score",
    )(*records, *tables, *packed, *prev)


def exchange(value, axis, size, mask):
    return lax.ppermute(value, axis, [(i, i ^ mask) for i in range(size)])


def on_device(mesh_shape, record, templates, offsets, counts):
    blk = mesh_shape["blk"]
    taps = templates.shape[2]
    shifts = record.shape[2] - taps + 1
    packed, own = pack(templates[0], offsets, counts)
    mine = jnp.transpose(record[0])
    period = -(-record.shape[2] // 64) * 64
    tables = tuple(jnp.asarray(table) for table in fourier_tables(period, shifts))
    if blk == CHUNK:
        held = {0: own}
        held[4] = exchange(packed, "blk", blk, 4)
        theirs = exchange(mine, "chan", 2, 1)

        def step(masks, rows, last=False, split=False):
            return score(
                (mine, theirs), tables, [held[m] for m in masks], [(m, False) for m in masks],
                blk, taps, shifts, rows, last, split,
            )

        *rows, forward, inverse = step((0,), (), split=True)
        tables = (forward, inverse)
        rows, packed = lax.optimization_barrier((rows[0], packed))
        held[2] = exchange(packed, "blk", blk, 2)
        held[1] = exchange(packed, "blk", blk, 1)
        held[6] = exchange(held[4], "blk", blk, 2)
        held[5] = exchange(held[4], "blk", blk, 1)
        held[3] = exchange(held[1], "blk", blk, 2)
        rows = step((1, 2, 4), (rows,))
        rows, held[6] = lax.optimization_barrier((rows[0], held[6]))
        held[7] = exchange(held[6], "blk", blk, 1)
        rows = step((3, 5, 6), (rows,))
        rows = step((7,), rows, True)
        keep, send = rows
    else:
        theirs = exchange(mine, "chan", 2, 1)
        every = lax.all_gather(packed, "blk", axis=0, tiled=False)
        keeps, sends = [], []
        for at in range(0, blk, CHUNK):
            size = min(CHUNK, blk - at)
            keep, send, *_ = score(
                (mine, theirs), tables, [every[at + i] for i in range(size)],
                [(i, True) for i in range(size)], size, taps, shifts,
            )
            keeps.append(keep)
            sends.append(send)
        keep, send = jnp.concatenate(keeps, axis=0), jnp.concatenate(sends, axis=0)
    return (keep + exchange(send, "chan", 2, 1))[None]


def solution(mesh):
    in_specs = (P(("grp", "blk"), "chan", None), P("blk", "chan", None), P("blk"), P("blk"))
    out_specs = P(("grp", "blk"), None, "chan")
    return jax.shard_map(
        functools.partial(on_device, dict(mesh.shape)),
        mesh=mesh, in_specs=in_specs, out_specs=out_specs, check_vma=False,
    )
```

```python
import functools

import jax
import jax.numpy as jnp
import numpy as np
from jax import lax
from jax.experimental import pallas as pl
from jax.experimental.pallas import tpu as pltpu
from jax.sharding import PartitionSpec as P

LANES = 128
META = 8
CHUNK = 8
PITCH = 9


def pack_kernel(off_ref, cnt_ref, tmpl_ref, out_ref, own_ref):
    rows, taps = tmpl_ref.shape
    lane = lax.broadcasted_iota(jnp.int32, (META, rows), 1)
    level = lax.broadcasted_iota(jnp.int32, (META, rows), 0)
    value = jnp.where(lane == 0, off_ref[0], cnt_ref[0])
    meta = jnp.where(level == 0, value >> 8, value & 255).astype(jnp.float32).astype(out_ref.dtype)
    turned = jnp.transpose(tmpl_ref[...].astype(jnp.float32)).astype(out_ref.dtype)
    for ref in (out_ref, own_ref):
        ref[:taps, :] = turned
        ref[taps:, :] = meta


def pack(templates, offsets, counts):
    rows, taps = templates.shape
    smem = pl.BlockSpec(memory_space=pltpu.SMEM)
    vmem = pl.BlockSpec(memory_space=pltpu.VMEM)
    return pl.pallas_call(
        pack_kernel,
        out_shape=(jax.ShapeDtypeStruct((taps + META, rows), templates.dtype),) * 2,
        in_specs=[smem, smem, vmem],
        out_specs=(vmem, vmem),
        cost_estimate=pl.CostEstimate(flops=4 * 10**9, bytes_accessed=10**7, transcendentals=0),
        compiler_params=pltpu.CompilerParams(vmem_limit_bytes=4 * 2**20),
        name="pack",
    )(offsets, counts, templates)


def three_terms(value):
    terms = []
    for _ in range(3):
        terms.append(value.astype(jnp.bfloat16))
        value = value - terms[-1].astype(jnp.float32)
    return terms


def fourier_tables(period, shifts):
    bins = -(-(period // 2 + 1) // 8) * 8
    k = np.arange(bins)[:, None]
    used = k <= period // 2
    angle = 2 * np.pi * k * np.arange(period)[None, :] / period
    forward = np.concatenate([np.cos(angle) * used, np.sin(angle) * used], axis=0)
    weight = np.where((k == 0) | (k == period // 2), 1.0, 2.0) / period
    inverse = np.concatenate([forward[:bins] * weight, -forward[bins:] * weight], axis=0)
    return forward.astype(np.float32), inverse[:, :shifts].T.astype(np.float32)


def score_kernel(taps, shifts, places, more, last, split, *refs):
    n = len(places)
    mine, theirs, forward, inverse = refs[:4]
    packed = refs[4 : 4 + n]
    at = 4 + n + more
    prev_ref, outs = refs[4 + n : at], refs[at : at + 1 + last + 2 * split]
    gains, ints, tails, rows_f, rows_b, sums, scales = refs[at + len(outs) :]
    samples, channels = mine.shape
    width = packed[0].shape[1]
    groups = width // LANES
    whole_tiles = channels // LANES
    rest = channels - whole_tiles * LANES
    chan = lax.axis_index("chan")
    blocks = shifts // 8
    steps = taps // 8
    lane_row = lax.broadcasted_iota(jnp.int32, (1, LANES), 1)

    for i in range(n):
        meta = packed[i][taps:, :LANES].astype(jnp.float32)
        numbers = (meta[:1] * 256.0 + meta[1:2]).astype(jnp.int32)
        ints[i, 0] = numbers[0, 0]
        ints[i, 1] = numbers[0, 1]
    for i in range(n):
        for g in range(groups):
            block = packed[i][:taps, g * LANES : (g + 1) * LANES].astype(jnp.float32)
            tiles = [block[8 * a : 8 * a + 8] for a in range(steps)]
            energy = jnp.zeros((8, LANES), jnp.float32)
            for a in range(0, steps, 2):
                energy = energy + (tiles[a] * tiles[a] + tiles[a + 1] * tiles[a + 1])
            gains[i * groups + g : i * groups + g + 1, :] = jnp.sum(energy, axis=0, keepdims=True)
    if rest:
        tails[0, :, :rest] = mine[:, whole_tiles * LANES :]
        tails[1, :, :rest] = theirs[:, whole_tiles * LANES :]
    rows_f[:, (samples // 8) * 8 :, :] = jnp.zeros_like(rows_f[:, (samples // 8) * 8 :, :])
    for i in range(n):
        count = jnp.full((1, LANES), ints[i, 1], jnp.int32)
        ratio = lax.rsqrt(count.astype(jnp.float32)) * (taps**0.5 / taps)
        for g in range(groups):
            at = i * groups + g
            gain = lax.rsqrt(gains[at : at + 1, :] * (1.0 / taps) + 1e-06) * ratio
            gains[at : at + 1, :] = jnp.where(lane_row + (chan * width + g * LANES) < count, gain, 0.0)

    wide = lax.broadcasted_iota(jnp.int32, (samples, LANES), 1)

    def turned(low, high, turn):
        mixed = jnp.where(wide < turn, high.astype(jnp.float32), low.astype(jnp.float32))
        return pltpu.roll(mixed, (LANES - turn) & (LANES - 1), 1)

    def item(i, _):
        first = ints[i, 0] + chan * width
        half = jnp.where(first < channels, 0, 1)
        local = first - half * channels
        tile = local >> 7
        fast = ((first + width <= channels) | (first >= channels)) & (tile + groups < whole_tiles)

        for source, here in ((mine, half == chan), (theirs, half != chan)):

            @pl.when(fast & here)
            def _():
                found = [
                    source[:, pl.ds(pl.multiple_of((tile + m) * LANES, LANES), LANES)].astype(jnp.float32)
                    for m in range(groups + 1)
                ]
                for g in range(groups):
                    rows_f[g, :samples, :] = turned(found[g], found[g + 1], local & (LANES - 1))

        @pl.when(jnp.logical_not(fast))
        def _():
            for g in range(groups):
                sides = []
                for side in range(2):
                    begin = first + g * LANES - side * channels
                    found = []
                    for m in range(2):
                        want = (begin >> 7) + m
                        at = pl.multiple_of(jnp.clip(want, 0, whole_tiles - 1) * LANES, LANES)
                        value = jnp.where(
                            chan == side,
                            mine[:, pl.ds(at, LANES)].astype(jnp.float32),
                            theirs[:, pl.ds(at, LANES)].astype(jnp.float32),
                        )
                        if rest:
                            tail = tails[jnp.where(chan == side, 0, 1)].astype(jnp.float32)
                            value = jnp.where(want >= whole_tiles, tail, value)
                        found.append(value)
                    sides.append(turned(found[0], found[1], begin & (LANES - 1)))
                split = channels - first - g * LANES
                rows_f[g, :samples, :] = jnp.where(wide < split, sides[0], sides[1])

        origin = i >> 16
        for g in range(groups):
            index = i * groups + g
            rows_b[i, :, g * LANES : (g + 1) * LANES] = rows_f[g].astype(jnp.bfloat16)

            level = [rows_f[g, 8 * m : 8 * m + 8, :] for m in range(steps + blocks)]
            level = [v * v for v in level]
            span = 1
            while span < steps:
                level = [level[m] + level[m + span] for m in range(len(level) - span)]
                span *= 2
            for m in range(blocks + 1):
                sums[g, pl.ds(origin + PITCH * m, 8), :] = level[m]
            near = [sums[g, pl.ds(m + m // 8, 8, stride=PITCH), :] for m in range(15)]
            before, after = [near[7]], [near[8]]
            for m in range(1, 8):
                before.append(before[-1] + near[7 - m])
            for m in range(1, 7):
                after.append(after[-1] + near[8 + m])
            window = [before[7]] + [before[7 - b] + after[b - 1] for b in range(1, 8)]
            gain = gains[pl.ds(index, 8, stride=0), :]
            for b in range(8):
                scale = lax.rsqrt(window[b] * (1.0 / taps) + 1e-06) * gain
                scales[pl.ds(index * shifts + b, 8, stride=8), :] = scale
        return 0

    lax.fori_loop(0, n, item, 0)

    def dot(left, right):
        return jnp.dot(left, right, preferred_element_type=jnp.float32)

    if split:
        for table, ref in zip((forward, inverse), outs[-2:]):
            ref[...] = jnp.concatenate(three_terms(table[...]), axis=0)
        forward, inverse = outs[-2:]
    tall = forward.shape[0] // 3
    bins = tall // 2
    totals = []
    for i in range(n):
        spectra = []
        for value, depth in ((rows_b[i], rows_b.shape[1]), (packed[i][:taps, :], taps)):
            terms = dot(forward[:, :depth], value)
            spectra.append(terms[2 * tall :] + terms[tall : 2 * tall] + terms[:tall])
        rec, tmpl = spectra
        rec_c, rec_s, tmpl_c, tmpl_s = rec[:bins], rec[bins:], tmpl[:bins], tmpl[bins:]
        spectrum = jnp.concatenate(
            [rec_c * tmpl_c + rec_s * tmpl_s, rec_c * tmpl_s - rec_s * tmpl_c], axis=0
        )
        products = [
            dot(inverse[: (3 - m) * shifts, :], term)
            for m, term in enumerate(three_terms(spectrum))
        ]
        small = products[0][2 * shifts :] + products[1][shifts:] + products[2]
        lag = small + (products[0][shifts : 2 * shifts] + products[1][:shifts]) + products[0][:shifts]
        totals.append(
            sum(
                lag[:, g * LANES : (g + 1) * LANES]
                * scales[(i * groups + g) * shifts : (i * groups + g + 1) * shifts, :]
                for g in range(groups)
            )
        )

    ones = jnp.ones((8, LANES), jnp.bfloat16)
    stacked = sum(
        lax.dot_general(ones, term, (((1,), (1,)), ((), ())), preferred_element_type=jnp.float32)
        for term in three_terms(jnp.concatenate(totals, axis=0))
    )
    result = prev_ref[0][...] if more else jnp.zeros(outs[0].shape[:1] + (shifts,), jnp.float32)
    sub = lax.broadcasted_iota(jnp.int32, result.shape, 0)
    blk = lax.axis_index("blk")
    for i in range(n):
        row = places[i][0] if places[i][1] else blk ^ places[i][0]
        result = jnp.where(sub == row, stacked[:1, i * shifts : (i + 1) * shifts], result)
    if not last:
        outs[0][...] = result
        return
    left, right = result[:, : shifts // 2], result[:, shifts // 2 :]
    outs[0][...] = jnp.where(chan == 0, left, right)
    outs[1][...] = jnp.where(chan == 0, right, left)


def score(records, tables, packed, places, templates, taps, shifts, prev=(), last=True, split=True):
    n = len(packed)
    samples, channels = records[0].shape
    width = packed[0].shape[1]
    groups = width // LANES
    items = n * groups
    padded = tables[0].shape[1]
    vmem = pl.BlockSpec(memory_space=pltpu.VMEM)
    if last:
        out_shape = (jax.ShapeDtypeStruct((templates, shifts // 2), jnp.float32),) * 2
    else:
        out_shape = (jax.ShapeDtypeStruct((templates, shifts), jnp.float32),)
    if split:
        out_shape += tuple(
            jax.ShapeDtypeStruct((3 * table.shape[0], table.shape[1]), jnp.bfloat16) for table in tables
        )
    return pl.pallas_call(
        functools.partial(score_kernel, taps, shifts, places, len(prev), int(last), int(split)),
        out_shape=out_shape,
        in_specs=[vmem] * (4 + n + len(prev)),
        out_specs=(vmem,) * len(out_shape),
        scratch_shapes=[
            pltpu.VMEM((-(-items // 8) * 8 + 8, LANES), jnp.float32),
            pltpu.SMEM((n, 2), jnp.int32),
            pltpu.VMEM((2, samples, LANES), records[0].dtype),
            pltpu.VMEM((groups, padded, LANES), jnp.float32),
            pltpu.VMEM((n, padded, width), jnp.bfloat16),
            pltpu.VMEM((groups, (shifts // 8 + 2) * PITCH, LANES), jnp.float32),
            pltpu.VMEM((items * shifts + 8, LANES), jnp.float32),
        ],
        compiler_params=pltpu.CompilerParams(vmem_limit_bytes=32 * 2**20),
        cost_estimate=pl.CostEstimate(
            flops=2 * n * width * taps * shifts, bytes_accessed=n * width * samples * 4, transcendentals=0
        ),
        name="score",
    )(*records, *tables, *packed, *prev)


def exchange(value, axis, size, mask):
    return lax.ppermute(value, axis, [(i, i ^ mask) for i in range(size)])


def on_device(mesh_shape, record, templates, offsets, counts):
    blk = mesh_shape["blk"]
    taps = templates.shape[2]
    shifts = record.shape[2] - taps + 1
    packed, own = pack(templates[0], offsets, counts)
    mine = jnp.transpose(record[0])
    period = -(-record.shape[2] // 64) * 64
    tables = tuple(jnp.asarray(table) for table in fourier_tables(period, shifts))
    if blk == CHUNK:
        held = {0: own}
        for mask in (4, 1, 2, 3):
            held[mask] = exchange(packed, "blk", blk, mask)
        theirs = exchange(mine, "chan", 2, 1)

        def step(masks, rows, last=False, split=False):
            return score(
                (mine, theirs), tables, [held[m] for m in masks], [(m, False) for m in masks],
                blk, taps, shifts, rows, last, split,
            )

        *rows, forward, inverse = step((0,), (), split=True)
        tables = (forward, inverse)
        near = lax.optimization_barrier((rows[0], *(held[m] for m in (3, 2, 1, 4))))
        held.update(zip((3, 2, 1, 4), near[1:]))
        held[6] = exchange(held[4], "blk", blk, 2)
        held[5] = exchange(held[4], "blk", blk, 1)
        rows = step((1, 2), near[:1])
        rows, held[6] = lax.optimization_barrier((rows[0], held[6]))
        held[7] = exchange(held[6], "blk", blk, 1)
        rows = step((3, 4, 5, 6), (rows,))
        rows = step((7,), rows, True)
        keep, send = rows
    else:
        theirs = exchange(mine, "chan", 2, 1)
        every = lax.all_gather(packed, "blk", axis=0, tiled=False)
        keeps, sends = [], []
        for at in range(0, blk, CHUNK):
            size = min(CHUNK, blk - at)
            keep, send, *_ = score(
                (mine, theirs), tables, [every[at + i] for i in range(size)],
                [(i, True) for i in range(size)], size, taps, shifts,
            )
            keeps.append(keep)
            sends.append(send)
        keep, send = jnp.concatenate(keeps, axis=0), jnp.concatenate(sends, axis=0)
    return (keep + exchange(send, "chan", 2, 1))[None]


def solution(mesh):
    in_specs = (P(("grp", "blk"), "chan", None), P("blk", "chan", None), P("blk"), P("blk"))
    out_specs = P(("grp", "blk"), None, "chan")
    return jax.shard_map(
        functools.partial(on_device, dict(mesh.shape)),
        mesh=mesh, in_specs=in_specs, out_specs=out_specs, check_vma=False,
    )
```

```python
import functools

import jax
import jax.numpy as jnp
import numpy as np
from jax import lax
from jax.experimental import pallas as pl
from jax.experimental.pallas import tpu as pltpu
from jax.sharding import PartitionSpec as P

LANES = 128
META = 8
CHUNK = 8
PITCH = 9


def pack_kernel(off_ref, cnt_ref, tmpl_ref, out_ref, own_ref):
    rows, taps = tmpl_ref.shape
    lane = lax.broadcasted_iota(jnp.int32, (META, rows), 1)
    level = lax.broadcasted_iota(jnp.int32, (META, rows), 0)
    value = jnp.where(lane == 0, off_ref[0], cnt_ref[0])
    meta = jnp.where(level == 0, value >> 8, value & 255).astype(jnp.float32).astype(out_ref.dtype)
    turned = jnp.transpose(tmpl_ref[...].astype(jnp.float32)).astype(out_ref.dtype)
    for ref in (out_ref, own_ref):
        ref[:taps, :] = turned
        ref[taps:, :] = meta


def pack(templates, offsets, counts):
    rows, taps = templates.shape
    smem = pl.BlockSpec(memory_space=pltpu.SMEM)
    vmem = pl.BlockSpec(memory_space=pltpu.VMEM)
    return pl.pallas_call(
        pack_kernel,
        out_shape=(jax.ShapeDtypeStruct((taps + META, rows), templates.dtype),) * 2,
        in_specs=[smem, smem, vmem],
        out_specs=(vmem, vmem),
        cost_estimate=pl.CostEstimate(flops=4 * 10**9, bytes_accessed=10**7, transcendentals=0),
        compiler_params=pltpu.CompilerParams(vmem_limit_bytes=4 * 2**20),
        name="pack",
    )(offsets, counts, templates)


def three_terms(value):
    terms = []
    for _ in range(3):
        terms.append(value.astype(jnp.bfloat16))
        value = value - terms[-1].astype(jnp.float32)
    return terms


def fourier_tables(period, shifts):
    bins = -(-(period // 2 + 1) // 8) * 8
    k = np.arange(bins)[:, None]
    used = k <= period // 2
    angle = 2 * np.pi * k * np.arange(period)[None, :] / period
    forward = np.concatenate([np.cos(angle) * used, np.sin(angle) * used], axis=0)
    weight = np.where((k == 0) | (k == period // 2), 1.0, 2.0) / period
    inverse = np.concatenate([forward[:bins] * weight, -forward[bins:] * weight], axis=0)
    return forward.astype(np.float32), inverse[:, :shifts].T.astype(np.float32)


def score_kernel(taps, shifts, places, more, last, split, *refs):
    n = len(places)
    mine, theirs, forward, inverse = refs[:4]
    packed = refs[4 : 4 + n]
    at = 4 + n + more
    prev_ref, outs = refs[4 + n : at], refs[at : at + 1 + last + 2 * split]
    gains, ints, tails, rows_f, rows_b, sums, scales = refs[at + len(outs) :]
    samples, channels = mine.shape
    width = packed[0].shape[1]
    groups = width // LANES
    whole_tiles = channels // LANES
    rest = channels - whole_tiles * LANES
    chan = lax.axis_index("chan")
    blocks = shifts // 8
    steps = taps // 8
    lane_row = lax.broadcasted_iota(jnp.int32, (1, LANES), 1)

    for i in range(n):
        meta = packed[i][taps:, :LANES].astype(jnp.float32)
        numbers = (meta[:1] * 256.0 + meta[1:2]).astype(jnp.int32)
        ints[i, 0] = numbers[0, 0]
        ints[i, 1] = numbers[0, 1]
    for i in range(n):
        for g in range(groups):
            block = packed[i][:taps, g * LANES : (g + 1) * LANES].astype(jnp.float32)
            tiles = [block[8 * a : 8 * a + 8] for a in range(steps)]
            energy = jnp.zeros((8, LANES), jnp.float32)
            for a in range(0, steps, 2):
                energy = energy + (tiles[a] * tiles[a] + tiles[a + 1] * tiles[a + 1])
            gains[i * groups + g : i * groups + g + 1, :] = jnp.sum(energy, axis=0, keepdims=True)
    if rest:
        tails[0, :, :rest] = mine[:, whole_tiles * LANES :]
        tails[1, :, :rest] = theirs[:, whole_tiles * LANES :]
    rows_f[:, (samples // 8) * 8 :, :] = jnp.zeros_like(rows_f[:, (samples // 8) * 8 :, :])
    for i in range(n):
        count = jnp.full((1, LANES), ints[i, 1], jnp.int32)
        ratio = lax.rsqrt(count.astype(jnp.float32)) * (taps**0.5 / taps)
        for g in range(groups):
            at = i * groups + g
            gain = lax.rsqrt(gains[at : at + 1, :] * (1.0 / taps) + 1e-06) * ratio
            gains[at : at + 1, :] = jnp.where(lane_row + (chan * width + g * LANES) < count, gain, 0.0)

    wide = lax.broadcasted_iota(jnp.int32, (samples, LANES), 1)

    def turned(low, high, turn):
        mixed = jnp.where(wide < turn, high.astype(jnp.float32), low.astype(jnp.float32))
        return pltpu.roll(mixed, (LANES - turn) & (LANES - 1), 1)

    def item(i, _):
        first = ints[i, 0] + chan * width
        half = jnp.where(first < channels, 0, 1)
        local = first - half * channels
        tile = local >> 7
        fast = ((first + width <= channels) | (first >= channels)) & (tile + groups < whole_tiles)

        for source, here in ((mine, half == chan), (theirs, half != chan)):

            @pl.when(fast & here)
            def _():
                found = [
                    source[:, pl.ds(pl.multiple_of((tile + m) * LANES, LANES), LANES)].astype(jnp.float32)
                    for m in range(groups + 1)
                ]
                for g in range(groups):
                    rows_f[g, :samples, :] = turned(found[g], found[g + 1], local & (LANES - 1))

        @pl.when(jnp.logical_not(fast))
        def _():
            for g in range(groups):
                sides = []
                for side in range(2):
                    begin = first + g * LANES - side * channels
                    found = []
                    for m in range(2):
                        want = (begin >> 7) + m
                        at = pl.multiple_of(jnp.clip(want, 0, whole_tiles - 1) * LANES, LANES)
                        value = jnp.where(
                            chan == side,
                            mine[:, pl.ds(at, LANES)].astype(jnp.float32),
                            theirs[:, pl.ds(at, LANES)].astype(jnp.float32),
                        )
                        if rest:
                            tail = tails[jnp.where(chan == side, 0, 1)].astype(jnp.float32)
                            value = jnp.where(want >= whole_tiles, tail, value)
                        found.append(value)
                    sides.append(turned(found[0], found[1], begin & (LANES - 1)))
                split = channels - first - g * LANES
                rows_f[g, :samples, :] = jnp.where(wide < split, sides[0], sides[1])

        origin = i >> 16
        for g in range(groups):
            index = i * groups + g
            rows_b[i, :, g * LANES : (g + 1) * LANES] = rows_f[g].astype(jnp.bfloat16)

            level = [rows_f[g, 8 * m : 8 * m + 8, :] for m in range(steps + blocks)]
            level = [v * v for v in level]
            span = 1
            while span < steps:
                level = [level[m] + level[m + span] for m in range(len(level) - span)]
                span *= 2
            for m in range(blocks + 1):
                sums[g, pl.ds(origin + PITCH * m, 8), :] = level[m]
            near = [sums[g, pl.ds(m + m // 8, 8, stride=PITCH), :] for m in range(15)]
            before, after = [near[7]], [near[8]]
            for m in range(1, 8):
                before.append(before[-1] + near[7 - m])
            for m in range(1, 7):
                after.append(after[-1] + near[8 + m])
            window = [before[7]] + [before[7 - b] + after[b - 1] for b in range(1, 8)]
            gain = gains[pl.ds(index, 8, stride=0), :]
            for b in range(8):
                scale = lax.rsqrt(window[b] * (1.0 / taps) + 1e-06) * gain
                scales[pl.ds(index * shifts + b, 8, stride=8), :] = scale
        return 0

    lax.fori_loop(0, n, item, 0)

    def dot(left, right):
        return jnp.dot(left, right, preferred_element_type=jnp.float32)

    if split:
        for table, ref in zip((forward, inverse), outs[-2:]):
            ref[...] = jnp.concatenate(three_terms(table[...]), axis=0)
        forward, inverse = outs[-2:]
    tall = forward.shape[0] // 3
    bins = tall // 2
    totals = []
    for i in range(n):
        spectra = []
        for value, depth in ((rows_b[i], rows_b.shape[1]), (packed[i][:taps, :], taps)):
            terms = dot(forward[:, :depth], value)
            spectra.append(terms[2 * tall :] + terms[tall : 2 * tall] + terms[:tall])
        rec, tmpl = spectra
        rec_c, rec_s, tmpl_c, tmpl_s = rec[:bins], rec[bins:], tmpl[:bins], tmpl[bins:]
        spectrum = jnp.concatenate(
            [rec_c * tmpl_c + rec_s * tmpl_s, rec_c * tmpl_s - rec_s * tmpl_c], axis=0
        )
        products = [
            dot(inverse[: (3 - m) * shifts, :], term)
            for m, term in enumerate(three_terms(spectrum))
        ]
        small = products[0][2 * shifts :] + products[1][shifts:] + products[2]
        lag = small + (products[0][shifts : 2 * shifts] + products[1][:shifts]) + products[0][:shifts]
        totals.append(
            sum(
                lag[:, g * LANES : (g + 1) * LANES]
                * scales[(i * groups + g) * shifts : (i * groups + g + 1) * shifts, :]
                for g in range(groups)
            )
        )

    ones = jnp.ones((8, LANES), jnp.bfloat16)
    stacked = sum(
        lax.dot_general(ones, term, (((1,), (1,)), ((), ())), preferred_element_type=jnp.float32)
        for term in three_terms(jnp.concatenate(totals, axis=0))
    )
    result = prev_ref[0][...] if more else jnp.zeros(outs[0].shape[:1] + (shifts,), jnp.float32)
    sub = lax.broadcasted_iota(jnp.int32, result.shape, 0)
    blk = lax.axis_index("blk")
    for i in range(n):
        row = places[i][0] if places[i][1] else blk ^ places[i][0]
        result = jnp.where(sub == row, stacked[:1, i * shifts : (i + 1) * shifts], result)
    if not last:
        outs[0][...] = result
        return
    left, right = result[:, : shifts // 2], result[:, shifts // 2 :]
    outs[0][...] = jnp.where(chan == 0, left, right)
    outs[1][...] = jnp.where(chan == 0, right, left)


def score(records, tables, packed, places, templates, taps, shifts, prev=(), last=True, split=True):
    n = len(packed)
    samples, channels = records[0].shape
    width = packed[0].shape[1]
    groups = width // LANES
    items = n * groups
    padded = tables[0].shape[1]
    vmem = pl.BlockSpec(memory_space=pltpu.VMEM)
    if last:
        out_shape = (jax.ShapeDtypeStruct((templates, shifts // 2), jnp.float32),) * 2
    else:
        out_shape = (jax.ShapeDtypeStruct((templates, shifts), jnp.float32),)
    if split:
        out_shape += tuple(
            jax.ShapeDtypeStruct((3 * table.shape[0], table.shape[1]), jnp.bfloat16) for table in tables
        )
    return pl.pallas_call(
        functools.partial(score_kernel, taps, shifts, places, len(prev), int(last), int(split)),
        out_shape=out_shape,
        in_specs=[vmem] * (4 + n + len(prev)),
        out_specs=(vmem,) * len(out_shape),
        scratch_shapes=[
            pltpu.VMEM((-(-items // 8) * 8 + 8, LANES), jnp.float32),
            pltpu.SMEM((n, 2), jnp.int32),
            pltpu.VMEM((2, samples, LANES), records[0].dtype),
            pltpu.VMEM((groups, padded, LANES), jnp.float32),
            pltpu.VMEM((n, padded, width), jnp.bfloat16),
            pltpu.VMEM((groups, (shifts // 8 + 2) * PITCH, LANES), jnp.float32),
            pltpu.VMEM((items * shifts + 8, LANES), jnp.float32),
        ],
        compiler_params=pltpu.CompilerParams(vmem_limit_bytes=32 * 2**20),
        cost_estimate=pl.CostEstimate(
            flops=2 * n * width * taps * shifts, bytes_accessed=n * width * samples * 4, transcendentals=0
        ),
        name="score",
    )(*records, *tables, *packed, *prev)


def exchange(value, axis, size, mask):
    return lax.ppermute(value, axis, [(i, i ^ mask) for i in range(size)])


def on_device(mesh_shape, record, templates, offsets, counts):
    blk = mesh_shape["blk"]
    taps = templates.shape[2]
    shifts = record.shape[2] - taps + 1
    packed, own = pack(templates[0], offsets, counts)
    mine = jnp.transpose(record[0])
    period = -(-record.shape[2] // 64) * 64
    tables = tuple(jnp.asarray(table) for table in fourier_tables(period, shifts))
    if blk == CHUNK:
        held = {0: own}
        for mask in (4, 1, 2):
            held[mask] = exchange(packed, "blk", blk, mask)
        theirs = exchange(mine, "chan", 2, 1)

        def step(masks, rows, last=False, split=False):
            return score(
                (mine, theirs), tables, [held[m] for m in masks], [(m, False) for m in masks],
                blk, taps, shifts, rows, last, split,
            )

        *rows, forward, inverse = step((0,), (), split=True)
        tables = (forward, inverse)
        near = lax.optimization_barrier((rows[0], *(held[m] for m in (4, 1, 2))))
        held.update(zip((4, 1, 2), near[1:]))
        held[6] = exchange(held[4], "blk", blk, 2)
        held[5] = exchange(held[4], "blk", blk, 1)
        held[3] = exchange(held[1], "blk", blk, 2)
        held[7] = exchange(held[6], "blk", blk, 1)
        rows = step((1, 2, 4, 5, 6), near[:1])
        rows = step((3, 7), rows, True)
        keep, send = rows
    else:
        theirs = exchange(mine, "chan", 2, 1)
        every = lax.all_gather(packed, "blk", axis=0, tiled=False)
        keeps, sends = [], []
        for at in range(0, blk, CHUNK):
            size = min(CHUNK, blk - at)
            keep, send, *_ = score(
                (mine, theirs), tables, [every[at + i] for i in range(size)],
                [(i, True) for i in range(size)], size, taps, shifts,
            )
            keeps.append(keep)
            sends.append(send)
        keep, send = jnp.concatenate(keeps, axis=0), jnp.concatenate(sends, axis=0)
    return (keep + exchange(send, "chan", 2, 1))[None]


def solution(mesh):
    in_specs = (P(("grp", "blk"), "chan", None), P("blk", "chan", None), P("blk"), P("blk"))
    out_specs = P(("grp", "blk"), None, "chan")
    return jax.shard_map(
        functools.partial(on_device, dict(mesh.shape)),
        mesh=mesh, in_specs=in_specs, out_specs=out_specs, check_vma=False,
    )
```

```python
import functools

import jax
import jax.numpy as jnp
import numpy as np
from jax import lax
from jax.experimental import pallas as pl
from jax.experimental.pallas import tpu as pltpu
from jax.sharding import PartitionSpec as P

LANES = 128
META = 8
CHUNK = 8
PITCH = 9


def pack_kernel(off_ref, cnt_ref, tmpl_ref, out_ref, own_ref):
    rows, taps = tmpl_ref.shape
    lane = lax.broadcasted_iota(jnp.int32, (META, rows), 1)
    level = lax.broadcasted_iota(jnp.int32, (META, rows), 0)
    value = jnp.where(lane == 0, off_ref[0], cnt_ref[0])
    meta = jnp.where(level == 0, value >> 8, value & 255).astype(jnp.float32).astype(out_ref.dtype)
    turned = jnp.transpose(tmpl_ref[...].astype(jnp.float32)).astype(out_ref.dtype)
    for ref in (out_ref, own_ref):
        ref[:taps, :] = turned
        ref[taps:, :] = meta


def pack(templates, offsets, counts):
    rows, taps = templates.shape
    smem = pl.BlockSpec(memory_space=pltpu.SMEM)
    vmem = pl.BlockSpec(memory_space=pltpu.VMEM)
    return pl.pallas_call(
        pack_kernel,
        out_shape=(jax.ShapeDtypeStruct((taps + META, rows), templates.dtype),) * 2,
        in_specs=[smem, smem, vmem],
        out_specs=(vmem, vmem),
        cost_estimate=pl.CostEstimate(flops=4 * 10**9, bytes_accessed=10**7, transcendentals=0),
        compiler_params=pltpu.CompilerParams(vmem_limit_bytes=4 * 2**20),
        name="pack",
    )(offsets, counts, templates)


def three_terms(value):
    terms = []
    for _ in range(3):
        terms.append(value.astype(jnp.bfloat16))
        value = value - terms[-1].astype(jnp.float32)
    return terms


def fourier_tables(period, shifts):
    bins = -(-(period // 2 + 1) // 8) * 8
    k = np.arange(bins)[:, None]
    used = k <= period // 2
    angle = 2 * np.pi * k * np.arange(period)[None, :] / period
    forward = np.concatenate([np.cos(angle) * used, np.sin(angle) * used], axis=0)
    weight = np.where((k == 0) | (k == period // 2), 1.0, 2.0) / period
    inverse = np.concatenate([forward[:bins] * weight, -forward[bins:] * weight], axis=0)
    return forward.astype(np.float32), inverse[:, :shifts].T.astype(np.float32)


def score_kernel(taps, shifts, places, more, last, split, *refs):
    n = len(places)
    mine, theirs, forward, inverse = refs[:4]
    packed = refs[4 : 4 + n]
    at = 4 + n + more
    prev_ref, outs = refs[4 + n : at], refs[at : at + 1 + last + 2 * split]
    gains, ints, tails, rows_f, rows_b, sums, scales = refs[at + len(outs) :]
    samples, channels = mine.shape
    width = packed[0].shape[1]
    groups = width // LANES
    whole_tiles = channels // LANES
    rest = channels - whole_tiles * LANES
    chan = lax.axis_index("chan")
    blocks = shifts // 8
    steps = taps // 8
    lane_row = lax.broadcasted_iota(jnp.int32, (1, LANES), 1)

    for i in range(n):
        meta = packed[i][taps:, :LANES].astype(jnp.float32)
        numbers = (meta[:1] * 256.0 + meta[1:2]).astype(jnp.int32)
        ints[i, 0] = numbers[0, 0]
        ints[i, 1] = numbers[0, 1]
    for i in range(n):
        for g in range(groups):
            block = packed[i][:taps, g * LANES : (g + 1) * LANES].astype(jnp.float32)
            tiles = [block[8 * a : 8 * a + 8] for a in range(steps)]
            energy = jnp.zeros((8, LANES), jnp.float32)
            for a in range(0, steps, 2):
                energy = energy + (tiles[a] * tiles[a] + tiles[a + 1] * tiles[a + 1])
            gains[i * groups + g : i * groups + g + 1, :] = jnp.sum(energy, axis=0, keepdims=True)
    if rest:
        tails[0, :, :rest] = mine[:, whole_tiles * LANES :]
        tails[1, :, :rest] = theirs[:, whole_tiles * LANES :]
    rows_f[:, (samples // 8) * 8 :, :] = jnp.zeros_like(rows_f[:, (samples // 8) * 8 :, :])
    for i in range(n):
        count = jnp.full((1, LANES), ints[i, 1], jnp.int32)
        ratio = lax.rsqrt(count.astype(jnp.float32)) * (taps**0.5 / taps)
        for g in range(groups):
            at = i * groups + g
            gain = lax.rsqrt(gains[at : at + 1, :] * (1.0 / taps) + 1e-06) * ratio
            gains[at : at + 1, :] = jnp.where(lane_row + (chan * width + g * LANES) < count, gain, 0.0)

    wide = lax.broadcasted_iota(jnp.int32, (samples, LANES), 1)

    def turned(low, high, turn):
        mixed = jnp.where(wide < turn, high.astype(jnp.float32), low.astype(jnp.float32))
        return pltpu.roll(mixed, (LANES - turn) & (LANES - 1), 1)

    def item(i, _):
        first = ints[i, 0] + chan * width
        half = jnp.where(first < channels, 0, 1)
        local = first - half * channels
        tile = local >> 7
        fast = ((first + width <= channels) | (first >= channels)) & (tile + groups < whole_tiles)

        for source, here in ((mine, half == chan), (theirs, half != chan)):

            @pl.when(fast & here)
            def _():
                found = [
                    source[:, pl.ds(pl.multiple_of((tile + m) * LANES, LANES), LANES)].astype(jnp.float32)
                    for m in range(groups + 1)
                ]
                for g in range(groups):
                    rows_f[g, :samples, :] = turned(found[g], found[g + 1], local & (LANES - 1))

        @pl.when(jnp.logical_not(fast))
        def _():
            for g in range(groups):
                sides = []
                for side in range(2):
                    begin = first + g * LANES - side * channels
                    found = []
                    for m in range(2):
                        want = (begin >> 7) + m
                        at = pl.multiple_of(jnp.clip(want, 0, whole_tiles - 1) * LANES, LANES)
                        value = jnp.where(
                            chan == side,
                            mine[:, pl.ds(at, LANES)].astype(jnp.float32),
                            theirs[:, pl.ds(at, LANES)].astype(jnp.float32),
                        )
                        if rest:
                            tail = tails[jnp.where(chan == side, 0, 1)].astype(jnp.float32)
                            value = jnp.where(want >= whole_tiles, tail, value)
                        found.append(value)
                    sides.append(turned(found[0], found[1], begin & (LANES - 1)))
                split = channels - first - g * LANES
                rows_f[g, :samples, :] = jnp.where(wide < split, sides[0], sides[1])

        origin = i >> 16
        for g in range(groups):
            index = i * groups + g
            rows_b[i, :, g * LANES : (g + 1) * LANES] = rows_f[g].astype(jnp.bfloat16)

            level = [rows_f[g, 8 * m : 8 * m + 8, :] for m in range(steps + blocks)]
            level = [v * v for v in level]
            span = 1
            while span < steps:
                level = [level[m] + level[m + span] for m in range(len(level) - span)]
                span *= 2
            for m in range(blocks + 1):
                sums[g, pl.ds(origin + PITCH * m, 8), :] = level[m]
            near = [sums[g, pl.ds(m + m // 8, 8, stride=PITCH), :] for m in range(15)]
            before, after = [near[7]], [near[8]]
            for m in range(1, 8):
                before.append(before[-1] + near[7 - m])
            for m in range(1, 7):
                after.append(after[-1] + near[8 + m])
            window = [before[7]] + [before[7 - b] + after[b - 1] for b in range(1, 8)]
            gain = gains[pl.ds(index, 8, stride=0), :]
            for b in range(8):
                scale = lax.rsqrt(window[b] * (1.0 / taps) + 1e-06) * gain
                scales[pl.ds(index * shifts + b, 8, stride=8), :] = scale
        return 0

    lax.fori_loop(0, n, item, 0)

    def dot(left, right):
        return jnp.dot(left, right, preferred_element_type=jnp.float32)

    if split:
        for table, ref in zip((forward, inverse), outs[-2:]):
            ref[...] = jnp.concatenate(three_terms(table[...]), axis=0)
        forward, inverse = outs[-2:]
    tall = forward.shape[0] // 3
    bins = tall // 2
    totals = []
    for i in range(n):
        spectra = []
        for value, depth in ((rows_b[i], rows_b.shape[1]), (packed[i][:taps, :], taps)):
            terms = dot(forward[:, :depth], value)
            spectra.append(terms[2 * tall :] + terms[tall : 2 * tall] + terms[:tall])
        rec, tmpl = spectra
        rec_c, rec_s, tmpl_c, tmpl_s = rec[:bins], rec[bins:], tmpl[:bins], tmpl[bins:]
        spectrum = jnp.concatenate(
            [rec_c * tmpl_c + rec_s * tmpl_s, rec_c * tmpl_s - rec_s * tmpl_c], axis=0
        )
        products = [
            dot(inverse[: (3 - m) * shifts, :], term)
            for m, term in enumerate(three_terms(spectrum))
        ]
        small = products[0][2 * shifts :] + products[1][shifts:] + products[2]
        lag = small + (products[0][shifts : 2 * shifts] + products[1][:shifts]) + products[0][:shifts]
        totals.append(
            sum(
                lag[:, g * LANES : (g + 1) * LANES]
                * scales[(i * groups + g) * shifts : (i * groups + g + 1) * shifts, :]
                for g in range(groups)
            )
        )

    ones = jnp.ones((8, LANES), jnp.bfloat16)
    stacked = sum(
        lax.dot_general(ones, term, (((1,), (1,)), ((), ())), preferred_element_type=jnp.float32)
        for term in three_terms(jnp.concatenate(totals, axis=0))
    )
    result = prev_ref[0][...] if more else jnp.zeros(outs[0].shape[:1] + (shifts,), jnp.float32)
    sub = lax.broadcasted_iota(jnp.int32, result.shape, 0)
    blk = lax.axis_index("blk")
    for i in range(n):
        row = places[i][0] if places[i][1] else blk ^ places[i][0]
        result = jnp.where(sub == row, stacked[:1, i * shifts : (i + 1) * shifts], result)
    if not last:
        outs[0][...] = result
        return
    left, right = result[:, : shifts // 2], result[:, shifts // 2 :]
    outs[0][...] = jnp.where(chan == 0, left, right)
    outs[1][...] = jnp.where(chan == 0, right, left)


def score(records, tables, packed, places, templates, taps, shifts, prev=(), last=True, split=True):
    n = len(packed)
    samples, channels = records[0].shape
    width = packed[0].shape[1]
    groups = width // LANES
    items = n * groups
    padded = tables[0].shape[1]
    vmem = pl.BlockSpec(memory_space=pltpu.VMEM)
    if last:
        out_shape = (jax.ShapeDtypeStruct((templates, shifts // 2), jnp.float32),) * 2
    else:
        out_shape = (jax.ShapeDtypeStruct((templates, shifts), jnp.float32),)
    if split:
        out_shape += tuple(
            jax.ShapeDtypeStruct((3 * table.shape[0], table.shape[1]), jnp.bfloat16) for table in tables
        )
    return pl.pallas_call(
        functools.partial(score_kernel, taps, shifts, places, len(prev), int(last), int(split)),
        out_shape=out_shape,
        in_specs=[vmem] * (4 + n + len(prev)),
        out_specs=(vmem,) * len(out_shape),
        scratch_shapes=[
            pltpu.VMEM((-(-items // 8) * 8 + 8, LANES), jnp.float32),
            pltpu.SMEM((n, 2), jnp.int32),
            pltpu.VMEM((2, samples, LANES), records[0].dtype),
            pltpu.VMEM((groups, padded, LANES), jnp.float32),
            pltpu.VMEM((n, padded, width), jnp.bfloat16),
            pltpu.VMEM((groups, (shifts // 8 + 2) * PITCH, LANES), jnp.float32),
            pltpu.VMEM((items * shifts + 8, LANES), jnp.float32),
        ],
        compiler_params=pltpu.CompilerParams(vmem_limit_bytes=32 * 2**20),
        cost_estimate=pl.CostEstimate(
            flops=2 * n * width * taps * shifts, bytes_accessed=n * width * samples * 4, transcendentals=0
        ),
        name="score",
    )(*records, *tables, *packed, *prev)


def exchange(value, axis, size, mask):
    return lax.ppermute(value, axis, [(i, i ^ mask) for i in range(size)])


def on_device(mesh_shape, record, templates, offsets, counts):
    blk = mesh_shape["blk"]
    taps = templates.shape[2]
    shifts = record.shape[2] - taps + 1
    packed, own = pack(templates[0], offsets, counts)
    mine = jnp.transpose(record[0])
    period = -(-record.shape[2] // 64) * 64
    tables = tuple(jnp.asarray(table) for table in fourier_tables(period, shifts))
    if blk == CHUNK:
        held = {0: own}
        held[4] = exchange(packed, "blk", blk, 4)
        theirs = exchange(mine, "chan", 2, 1)

        def step(masks, rows, last=False, split=False):
            return score(
                (mine, theirs), tables, [held[m] for m in masks], [(m, False) for m in masks],
                blk, taps, shifts, rows, last, split,
            )

        *rows, forward, inverse = step((0,), (), split=True)
        tables = (forward, inverse)
        rows, packed = lax.optimization_barrier((rows[0], packed))
        held[2] = exchange(packed, "blk", blk, 2)
        held[1] = exchange(packed, "blk", blk, 1)
        held[6] = exchange(held[4], "blk", blk, 2)
        held[5] = exchange(held[4], "blk", blk, 1)
        held[3] = exchange(held[1], "blk", blk, 2)
        rows = step((1, 2), (rows,))
        rows, held[6] = lax.optimization_barrier((rows[0], held[6]))
        held[7] = exchange(held[6], "blk", blk, 1)
        rows = step((3, 4, 5, 6), (rows,))
        rows = step((7,), rows, True)
        keep, send = rows
    else:
        theirs = exchange(mine, "chan", 2, 1)
        every = lax.all_gather(packed, "blk", axis=0, tiled=False)
        keeps, sends = [], []
        for at in range(0, blk, CHUNK):
            size = min(CHUNK, blk - at)
            keep, send, *_ = score(
                (mine, theirs), tables, [every[at + i] for i in range(size)],
                [(i, True) for i in range(size)], size, taps, shifts,
            )
            keeps.append(keep)
            sends.append(send)
        keep, send = jnp.concatenate(keeps, axis=0), jnp.concatenate(sends, axis=0)
    return (keep + exchange(send, "chan", 2, 1))[None]


def solution(mesh):
    in_specs = (P(("grp", "blk"), "chan", None), P("blk", "chan", None), P("blk"), P("blk"))
    out_specs = P(("grp", "blk"), None, "chan")
    return jax.shard_map(
        functools.partial(on_device, dict(mesh.shape)),
        mesh=mesh, in_specs=in_specs, out_specs=out_specs, check_vma=False,
    )
```

```python
import functools

import jax
import jax.numpy as jnp
import numpy as np
from jax import lax
from jax.experimental import pallas as pl
from jax.experimental.pallas import tpu as pltpu
from jax.sharding import PartitionSpec as P

LANES = 128
META = 8
CHUNK = 8
PITCH = 9


def pack_kernel(off_ref, cnt_ref, tmpl_ref, out_ref, own_ref):
    rows, taps = tmpl_ref.shape
    lane = lax.broadcasted_iota(jnp.int32, (META, rows), 1)
    level = lax.broadcasted_iota(jnp.int32, (META, rows), 0)
    value = jnp.where(lane == 0, off_ref[0], cnt_ref[0])
    meta = jnp.where(level == 0, value >> 8, value & 255).astype(jnp.float32).astype(out_ref.dtype)
    turned = jnp.transpose(tmpl_ref[...].astype(jnp.float32)).astype(out_ref.dtype)
    for ref in (out_ref, own_ref):
        ref[:taps, :] = turned
        ref[taps:, :] = meta


def pack(templates, offsets, counts):
    rows, taps = templates.shape
    smem = pl.BlockSpec(memory_space=pltpu.SMEM)
    vmem = pl.BlockSpec(memory_space=pltpu.VMEM)
    return pl.pallas_call(
        pack_kernel,
        out_shape=(jax.ShapeDtypeStruct((taps + META, rows), templates.dtype),) * 2,
        in_specs=[smem, smem, vmem],
        out_specs=(vmem, vmem),
        cost_estimate=pl.CostEstimate(flops=4 * 10**9, bytes_accessed=10**7, transcendentals=0),
        compiler_params=pltpu.CompilerParams(vmem_limit_bytes=4 * 2**20),
        name="pack",
    )(offsets, counts, templates)


def three_terms(value):
    terms = []
    for _ in range(3):
        terms.append(value.astype(jnp.bfloat16))
        value = value - terms[-1].astype(jnp.float32)
    return terms


def fourier_tables(period, shifts):
    bins = -(-(period // 2 + 1) // 8) * 8
    k = np.arange(bins)[:, None]
    used = k <= period // 2
    angle = 2 * np.pi * k * np.arange(period)[None, :] / period
    forward = np.concatenate([np.cos(angle) * used, np.sin(angle) * used], axis=0)
    weight = np.where((k == 0) | (k == period // 2), 1.0, 2.0) / period
    inverse = np.concatenate([forward[:bins] * weight, -forward[bins:] * weight], axis=0)
    return forward.astype(np.float32), inverse[:, :shifts].T.astype(np.float32)


def score_kernel(taps, shifts, places, more, last, split, *refs):
    n = len(places)
    mine, theirs, forward, inverse = refs[:4]
    packed = refs[4 : 4 + n]
    at = 4 + n + more
    prev_ref, outs = refs[4 + n : at], refs[at : at + 1 + last + 2 * split]
    gains, ints, tails, rows_f, rows_b, sums, scales = refs[at + len(outs) :]
    samples, channels = mine.shape
    width = packed[0].shape[1]
    groups = width // LANES
    whole_tiles = channels // LANES
    rest = channels - whole_tiles * LANES
    chan = lax.axis_index("chan")
    blocks = shifts // 8
    steps = taps // 8
    lane_row = lax.broadcasted_iota(jnp.int32, (1, LANES), 1)

    for i in range(n):
        meta = packed[i][taps:, :LANES].astype(jnp.float32)
        numbers = (meta[:1] * 256.0 + meta[1:2]).astype(jnp.int32)
        ints[i, 0] = numbers[0, 0]
        ints[i, 1] = numbers[0, 1]
    for i in range(n):
        for g in range(groups):
            block = packed[i][:taps, g * LANES : (g + 1) * LANES].astype(jnp.float32)
            tiles = [block[8 * a : 8 * a + 8] for a in range(steps)]
            energy = jnp.zeros((8, LANES), jnp.float32)
            for a in range(0, steps, 2):
                energy = energy + (tiles[a] * tiles[a] + tiles[a + 1] * tiles[a + 1])
            gains[i * groups + g : i * groups + g + 1, :] = jnp.sum(energy, axis=0, keepdims=True)
    if rest:
        tails[0, :, :rest] = mine[:, whole_tiles * LANES :]
        tails[1, :, :rest] = theirs[:, whole_tiles * LANES :]
    rows_f[:, (samples // 8) * 8 :, :] = jnp.zeros_like(rows_f[:, (samples // 8) * 8 :, :])
    for i in range(n):
        count = jnp.full((1, LANES), ints[i, 1], jnp.int32)
        ratio = lax.rsqrt(count.astype(jnp.float32)) * (taps**0.5 / taps)
        for g in range(groups):
            at = i * groups + g
            gain = lax.rsqrt(gains[at : at + 1, :] * (1.0 / taps) + 1e-06) * ratio
            gains[at : at + 1, :] = jnp.where(lane_row + (chan * width + g * LANES) < count, gain, 0.0)

    wide = lax.broadcasted_iota(jnp.int32, (samples, LANES), 1)

    def turned(low, high, turn):
        mixed = jnp.where(wide < turn, high.astype(jnp.float32), low.astype(jnp.float32))
        return pltpu.roll(mixed, (LANES - turn) & (LANES - 1), 1)

    def item(i, _):
        first = ints[i, 0] + chan * width
        half = jnp.where(first < channels, 0, 1)
        local = first - half * channels
        tile = local >> 7
        fast = ((first + width <= channels) | (first >= channels)) & (tile + groups < whole_tiles)

        for source, here in ((mine, half == chan), (theirs, half != chan)):

            @pl.when(fast & here)
            def _():
                found = [
                    source[:, pl.ds(pl.multiple_of((tile + m) * LANES, LANES), LANES)].astype(jnp.float32)
                    for m in range(groups + 1)
                ]
                for g in range(groups):
                    rows_f[g, :samples, :] = turned(found[g], found[g + 1], local & (LANES - 1))

        @pl.when(jnp.logical_not(fast))
        def _():
            for g in range(groups):
                sides = []
                for side in range(2):
                    begin = first + g * LANES - side * channels
                    found = []
                    for m in range(2):
                        want = (begin >> 7) + m
                        at = pl.multiple_of(jnp.clip(want, 0, whole_tiles - 1) * LANES, LANES)
                        value = jnp.where(
                            chan == side,
                            mine[:, pl.ds(at, LANES)].astype(jnp.float32),
                            theirs[:, pl.ds(at, LANES)].astype(jnp.float32),
                        )
                        if rest:
                            tail = tails[jnp.where(chan == side, 0, 1)].astype(jnp.float32)
                            value = jnp.where(want >= whole_tiles, tail, value)
                        found.append(value)
                    sides.append(turned(found[0], found[1], begin & (LANES - 1)))
                split = channels - first - g * LANES
                rows_f[g, :samples, :] = jnp.where(wide < split, sides[0], sides[1])

        origin = i >> 16
        for g in range(groups):
            index = i * groups + g
            rows_b[i, :, g * LANES : (g + 1) * LANES] = rows_f[g].astype(jnp.bfloat16)

            level = [rows_f[g, 8 * m : 8 * m + 8, :] for m in range(steps + blocks)]
            level = [v * v for v in level]
            span = 1
            while span < steps:
                level = [level[m] + level[m + span] for m in range(len(level) - span)]
                span *= 2
            for m in range(blocks + 1):
                sums[g, pl.ds(origin + PITCH * m, 8), :] = level[m]
            near = [sums[g, pl.ds(m + m // 8, 8, stride=PITCH), :] for m in range(15)]
            before, after = [near[7]], [near[8]]
            for m in range(1, 8):
                before.append(before[-1] + near[7 - m])
            for m in range(1, 7):
                after.append(after[-1] + near[8 + m])
            window = [before[7]] + [before[7 - b] + after[b - 1] for b in range(1, 8)]
            gain = gains[pl.ds(index, 8, stride=0), :]
            for b in range(8):
                scale = lax.rsqrt(window[b] * (1.0 / taps) + 1e-06) * gain
                scales[pl.ds(index * shifts + b, 8, stride=8), :] = scale
        return 0

    lax.fori_loop(0, n, item, 0)

    def dot(left, right):
        return jnp.dot(left, right, preferred_element_type=jnp.float32)

    if split:
        for table, ref in zip((forward, inverse), outs[-2:]):
            ref[...] = jnp.concatenate(three_terms(table[...]), axis=0)
        forward, inverse = outs[-2:]
    tall = forward.shape[0] // 3
    bins = tall // 2
    totals = []
    for i in range(n):
        spectra = []
        for value, depth in ((rows_b[i], rows_b.shape[1]), (packed[i][:taps, :], taps)):
            terms = dot(forward[:, :depth], value)
            spectra.append(terms[2 * tall :] + terms[tall : 2 * tall] + terms[:tall])
        rec, tmpl = spectra
        rec_c, rec_s, tmpl_c, tmpl_s = rec[:bins], rec[bins:], tmpl[:bins], tmpl[bins:]
        spectrum = jnp.concatenate(
            [rec_c * tmpl_c + rec_s * tmpl_s, rec_c * tmpl_s - rec_s * tmpl_c], axis=0
        )
        products = [
            dot(inverse[: (3 - m) * shifts, :], term)
            for m, term in enumerate(three_terms(spectrum))
        ]
        small = products[0][2 * shifts :] + products[1][shifts:] + products[2]
        lag = small + (products[0][shifts : 2 * shifts] + products[1][:shifts]) + products[0][:shifts]
        totals.append(
            sum(
                lag[:, g * LANES : (g + 1) * LANES]
                * scales[(i * groups + g) * shifts : (i * groups + g + 1) * shifts, :]
                for g in range(groups)
            )
        )

    ones = jnp.ones((8, LANES), jnp.bfloat16)
    stacked = sum(
        lax.dot_general(ones, term, (((1,), (1,)), ((), ())), preferred_element_type=jnp.float32)
        for term in three_terms(jnp.concatenate(totals, axis=0))
    )
    result = prev_ref[0][...] if more else jnp.zeros(outs[0].shape[:1] + (shifts,), jnp.float32)
    sub = lax.broadcasted_iota(jnp.int32, result.shape, 0)
    blk = lax.axis_index("blk")
    for i in range(n):
        row = places[i][0] if places[i][1] else blk ^ places[i][0]
        result = jnp.where(sub == row, stacked[:1, i * shifts : (i + 1) * shifts], result)
    if not last:
        outs[0][...] = result
        return
    left, right = result[:, : shifts // 2], result[:, shifts // 2 :]
    outs[0][...] = jnp.where(chan == 0, left, right)
    outs[1][...] = jnp.where(chan == 0, right, left)


def score(records, tables, packed, places, templates, taps, shifts, prev=(), last=True, split=True):
    n = len(packed)
    samples, channels = records[0].shape
    width = packed[0].shape[1]
    groups = width // LANES
    items = n * groups
    padded = tables[0].shape[1]
    vmem = pl.BlockSpec(memory_space=pltpu.VMEM)
    if last:
        out_shape = (jax.ShapeDtypeStruct((templates, shifts // 2), jnp.float32),) * 2
    else:
        out_shape = (jax.ShapeDtypeStruct((templates, shifts), jnp.float32),)
    if split:
        out_shape += tuple(
            jax.ShapeDtypeStruct((3 * table.shape[0], table.shape[1]), jnp.bfloat16) for table in tables
        )
    return pl.pallas_call(
        functools.partial(score_kernel, taps, shifts, places, len(prev), int(last), int(split)),
        out_shape=out_shape,
        in_specs=[vmem] * (4 + n + len(prev)),
        out_specs=(vmem,) * len(out_shape),
        scratch_shapes=[
            pltpu.VMEM((-(-items // 8) * 8 + 8, LANES), jnp.float32),
            pltpu.SMEM((n, 2), jnp.int32),
            pltpu.VMEM((2, samples, LANES), records[0].dtype),
            pltpu.VMEM((groups, padded, LANES), jnp.float32),
            pltpu.VMEM((n, padded, width), jnp.bfloat16),
            pltpu.VMEM((groups, (shifts // 8 + 2) * PITCH, LANES), jnp.float32),
            pltpu.VMEM((items * shifts + 8, LANES), jnp.float32),
        ],
        compiler_params=pltpu.CompilerParams(vmem_limit_bytes=32 * 2**20),
        cost_estimate=pl.CostEstimate(
            flops=2 * n * width * taps * shifts, bytes_accessed=n * width * samples * 4, transcendentals=0
        ),
        name="score",
    )(*records, *tables, *packed, *prev)


def exchange(value, axis, size, mask):
    return lax.ppermute(value, axis, [(i, i ^ mask) for i in range(size)])


def on_device(mesh_shape, record, templates, offsets, counts):
    blk = mesh_shape["blk"]
    taps = templates.shape[2]
    shifts = record.shape[2] - taps + 1
    packed, own = pack(templates[0], offsets, counts)
    mine = jnp.transpose(record[0])
    period = -(-record.shape[2] // 64) * 64
    tables = tuple(jnp.asarray(table) for table in fourier_tables(period, shifts))
    if blk == CHUNK:
        held = {0: own}
        held[4] = exchange(packed, "blk", blk, 4)
        held[1] = exchange(packed, "blk", blk, 1)
        theirs = exchange(mine, "chan", 2, 1)

        def step(masks, rows, last=False, split=False):
            return score(
                (mine, theirs), tables, [held[m] for m in masks], [(m, False) for m in masks],
                blk, taps, shifts, rows, last, split,
            )

        *rows, forward, inverse = step((0,), (), split=True)
        tables = (forward, inverse)
        rows, packed = lax.optimization_barrier((rows[0], packed))
        held[2] = exchange(packed, "blk", blk, 2)
        held[6] = exchange(held[4], "blk", blk, 2)
        held[5] = exchange(held[4], "blk", blk, 1)
        held[3] = exchange(held[1], "blk", blk, 2)
        rows = step((1, 2, 3), (rows,))
        rows, held[6] = lax.optimization_barrier((rows[0], held[6]))
        held[7] = exchange(held[6], "blk", blk, 1)
        rows = step((4, 5, 6), (rows,))
        rows = step((7,), rows, True)
        keep, send = rows
    else:
        theirs = exchange(mine, "chan", 2, 1)
        every = lax.all_gather(packed, "blk", axis=0, tiled=False)
        keeps, sends = [], []
        for at in range(0, blk, CHUNK):
            size = min(CHUNK, blk - at)
            keep, send, *_ = score(
                (mine, theirs), tables, [every[at + i] for i in range(size)],
                [(i, True) for i in range(size)], size, taps, shifts,
            )
            keeps.append(keep)
            sends.append(send)
        keep, send = jnp.concatenate(keeps, axis=0), jnp.concatenate(sends, axis=0)
    return (keep + exchange(send, "chan", 2, 1))[None]


def solution(mesh):
    in_specs = (P(("grp", "blk"), "chan", None), P("blk", "chan", None), P("blk"), P("blk"))
    out_specs = P(("grp", "blk"), None, "chan")
    return jax.shard_map(
        functools.partial(on_device, dict(mesh.shape)),
        mesh=mesh, in_specs=in_specs, out_specs=out_specs, check_vma=False,
    )
```
